256 devices in a mesh: ctx: 8 (over x, core), tp: 32 (over z, y).
Axes of the slice: x: 4, y: 4, z: 8, core: 2. Of those that a mesh axis runs over, the one named last changes fastest.
Arguments:
- streams: bfloat16 [16384, 3, 4096], P('ctx', None, 'tp'), may hold values from -6 to 6
- short_filter: float32 [3, 3, 4096], P(None, None, 'tp'), may hold values from -4 to 4
- residue: float32 [16, 4096], P(None, 'tp'), may hold values from -1.5 to 1.5
- decay_rate: float32 [16, 4096], P(None, 'tp'), may hold values from 1.8310547e-05 to 0.1
- skip_gain: float32 [4096], P('tp'), may hold values from -4 to 4
- out_weight: bfloat16 [4096, 4096], P(None, 'tp'), may hold values from -0.09375 to 0.09375
Outputs:
- projected: bfloat16 [16384, 4096], P('ctx', 'tp')
The draws below stay inside these ranges and needn't reach their ends.
All inputs are finite; a program needn't handle non-finite values.
Results may differ from the reference program's by a relative error of at most 0.0065.
Values may be sent and summed in bfloat16 or wider, within the bound.
No kernel may reach another device: no remote copies, remote signals or barrier semaphores. Data moves between devices by JAX's collectives and lax.ppermute only.
A program may use at most 128 MiB of HBM per device.

```python
import math
import jax
import jax.numpy as jnp
from jax import lax

D = 4096
ORDER = 16
SHORT = 3
SEQ = 16384


def draw_decay_rate(key, part):
    key = jax.random.fold_in(key, 7)
    key_pick, key_slow, key_fast = jax.random.split(key, 3)
    slow_share = 0.5
    shape = (ORDER, D)
    picked = jax.random.uniform(key_pick, shape, jnp.float32) < slow_share
    slow_log = jax.random.uniform(key_slow, shape, jnp.float32, math.log(0.3 / SEQ), math.log(2.0 / SEQ))
    fast_log = jax.random.uniform(key_fast, shape, jnp.float32, math.log(0.02), math.log(0.1))
    rates = jnp.exp(jnp.where(picked, slow_log, fast_log))
    return jnp.clip(rates, 0.3 / SEQ, 0.1).astype(jnp.float32)


def level_of(stream_key, dims, shards, low, top_value):
    factor_of = 1.0
    for axis_at, parts in shards:
        draws = jax.random.uniform(jax.random.fold_in(jax.random.fold_in(stream_key, 6), axis_at), (parts,), jnp.float32, low / len(shards), top_value / len(shards))
        factor_of = factor_of * jnp.repeat(jnp.exp(draws), dims[axis_at] // parts).reshape((-1,) + (1,) * (len(dims) - 1 - axis_at))
    return factor_of


def bell_draw(stream_key, dims, scale, bound, cuts=(), kind=jnp.bfloat16):
    result = jax.random.normal(stream_key, dims, jnp.float32) * scale
    if len(cuts) > 0:
        result = level_of(stream_key, dims, cuts, -0.22, 0.18) * result
    return jnp.clip(result, min=-bound, max=bound).astype(kind)


def setup_inputs(seed: int = 0) -> dict:
    streams_of = jax.random.split(jax.random.key(seed), 7)
    return {
        "streams": bell_draw(streams_of[0], (SEQ, 3, D), 1.0, 6.0, ((0, 8), (2, 32))),
        "short_filter": bell_draw(streams_of[1], (SHORT, 3, D), 0.6, 4.0, ((2, 32),), jnp.float32),
        "residue": bell_draw(streams_of[2], (ORDER, D), 0.25, 1.5, ((1, 32),), jnp.float32),
        "decay_rate": draw_decay_rate(jax.random.fold_in(streams_of[6], 71), 0),
        "skip_gain": bell_draw(streams_of[4], (D,), 1.0, 4.0, ((0, 32),), jnp.float32),
        "out_weight": bell_draw(streams_of[5], (D, D), D ** -0.5, 0.09375, ((1, 32),)),
    }


def featurize(streams, short_filter):
    padded = jnp.pad(streams.astype(jnp.float32), ((SHORT - 1, 0), (0, 0), (0, 0)))
    feat = jnp.zeros(streams.shape, jnp.float32)
    for tap_index in range(SHORT):
        feat = feat + short_filter[tap_index][None] * padded[tap_index:tap_index + SEQ]
    return feat

def convolve_group(operands):
    signal_rows, residue_rows, rate_rows = operands
    positions = jnp.arange(SEQ, dtype=jnp.float32)
    weights = residue_rows * jnp.sqrt(2.0 * rate_rows)
    filt = lax.optimization_barrier(jnp.sum(weights[:, :, None] * jnp.exp(-rate_rows[:, :, None] * positions[None, None, :]), axis=1))
    spectrum = jnp.fft.rfft(signal_rows, n=2 * SEQ, axis=1) * jnp.fft.rfft(filt, n=2 * SEQ, axis=1)
    return jnp.fft.irfft(spectrum, n=2 * SEQ, axis=1)[:, :SEQ]

def reference(streams, short_filter, residue, decay_rate, skip_gain, out_weight):
    feat = featurize(streams, short_filter)
    signal = feat[:, 1, :] * feat[:, 2, :]
    group_count = D // 128
    signal_groups = signal.T.reshape(group_count, 128, SEQ)
    residue_groups = residue.T.reshape(group_count, 128, ORDER)
    rate_groups = decay_rate.T.reshape(group_count, 128, ORDER)
    convolved = lax.map(convolve_group, (signal_groups, residue_groups, rate_groups))
    conv = convolved.reshape(D, SEQ).T + skip_gain[None, :] * signal
    gated = (feat[:, 0, :] * conv).astype(jnp.bfloat16)
    return jnp.dot(gated, out_weight, preferred_element_type=jnp.float32).astype(jnp.bfloat16)
```

```python
import jax
import jax.numpy as jnp
from jax import lax
from jax.experimental import pallas as pl
from jax.experimental.pallas import tpu as pltpu
from jax.sharding import Mesh, PartitionSpec as P

CTX = ("x", "core")
SUB = 8
PAD = 8
UNROLL = 8
PIECES = 2
ROW_TILE = 256


def shifted(value, axis, steps):
    count = lax.axis_size(axis)
    return lax.ppermute(value, axis, [(at, (at + steps) % count) for at in range(count)])


def from_behind(value, axis, steps):
    count = lax.axis_size(axis)
    return lax.ppermute(value, axis, [(at, at + steps) for at in range(count - steps)])


def wide(row):
    return jnp.broadcast_to(row, (SUB, row.shape[-1]))


def added(parts):
    while len(parts) > 1:
        pairs = [a + b for a, b in zip(parts[0::2], parts[1::2])]
        parts = pairs + parts[2 * len(pairs) :]
    return parts[0]


def unpack_stream(stream_ref, which, padded_ref):
    rows = stream_ref.shape[1]
    padded_ref[0:PAD, :] = jnp.zeros((PAD, padded_ref.shape[1]), jnp.float32)
    tile = 256

    def body(at, _):
        start = pl.multiple_of(at * tile, tile)
        block = stream_ref[which, pl.ds(start, tile), :].astype(jnp.float32)
        padded_ref[pl.ds(pl.multiple_of(PAD + at * tile, 8), tile), :] = block
        return 0

    lax.fori_loop(0, rows // tile, body, 0)


def state_kernel(stream_ref, taps_ref, rate_ref, signal_ref, start_ref, packed_ref, key_ref, val_ref):
    rows = stream_ref.shape[1]
    steps = rows // SUB
    order, chans = rate_ref.shape
    unpack_stream(stream_ref, 1, key_ref)
    unpack_stream(stream_ref, 2, val_ref)
    decay = [wide(jnp.exp(-rate_ref[r : r + 1, :])) for r in range(order)]
    key_taps = [wide(taps_ref[j, 1:2, :]) for j in range(3)]
    val_taps = [wide(taps_ref[j, 2:3, :]) for j in range(3)]
    block = lax.broadcasted_iota(jnp.int32, (SUB, chans), 0)

    def row(ref, step):
        return ref[pl.ds(PAD + step, SUB, stride=steps), :]

    def advance(step, carried, masked):
        k2, k1, v2, v1, *states = carried
        k0 = row(key_ref, step)
        v0 = row(val_ref, step)
        key = key_taps[0] * k2 + key_taps[1] * k1 + key_taps[2] * k0
        val = val_taps[0] * v2 + val_taps[1] * v1 + val_taps[2] * v0
        signal = key * val
        if masked:
            signal = jnp.where(block == 0, 0.0, signal)
        signal_ref[step] = signal
        states = [a * h + signal for a, h in zip(decay, states)]
        return [k1, k0, v1, v0, *states]

    carried = [row(key_ref, -2), row(key_ref, -1), row(val_ref, -2), row(val_ref, -1)]
    carried += [jnp.zeros((SUB, chans), jnp.float32)] * order
    for step in range(UNROLL):
        carried = advance(step, carried, step < 2)

    def body(at, carried):
        carried = list(carried)
        for step in range(UNROLL):
            carried = advance(at * UNROLL + step, carried, False)
        return tuple(carried)

    states = lax.fori_loop(1, steps // UNROLL, body, tuple(carried))[4:]
    for r in range(order):
        rate = wide(rate_ref[r : r + 1, :])
        total = states[r]
        for back in (1, 2, 4):
            gain = jnp.where(block >= back, jnp.exp(-rate * (steps * back)), 0.0)
            total = total + gain * pltpu.roll(total, back, 0)
        packed_ref[r : r + 1, :] = total[SUB - 1 : SUB, :]
        start_ref[r] = jnp.where(block == 0, 0.0, pltpu.roll(total, 1, 0))
    for s in range(3):
        head = stream_ref[s, 0:16, :].astype(jnp.float32)
        tail = stream_ref[s, rows - 16 : rows, :].astype(jnp.float32)
        packed_ref[order + 2 * s : order + 2 * s + 2, :] = head[0:2, :]
        packed_ref[order + 6 + 2 * s : order + 8 + 2 * s, :] = tail[14:16, :]
    packed_ref[order + 12 :, :] = jnp.zeros((packed_ref.shape[0] - order - 12, chans), jnp.float32)


def local_kernel(
    stream_ref, taps_ref, residue_ref, rate_ref, skip_ref, signal_ref, start_ref, query_ref, conv_ref, raw_ref
):
    rows = stream_ref.shape[1]
    steps = rows // SUB
    order, chans = rate_ref.shape
    unpack_stream(stream_ref, 0, raw_ref)
    decay = [wide(jnp.exp(-rate_ref[r : r + 1, :])) for r in range(order)]
    weight = [
        wide(residue_ref[r : r + 1, :] * jnp.sqrt(2.0 * rate_ref[r : r + 1, :])) for r in range(order)
    ]
    taps = [wide(taps_ref[j, 0:1, :]) for j in range(3)]
    skip = wide(skip_ref[0:1, :])

    def row(step):
        return raw_ref[pl.ds(PAD + step, SUB, stride=steps), :]

    def body(at, carried):
        q2, q1, *states = carried
        for inner in range(UNROLL):
            step = at * UNROLL + inner
            q0 = row(step)
            query_ref[step] = taps[0] * q2 + taps[1] * q1 + taps[2] * q0
            q2, q1 = q1, q0
            signal = signal_ref[step]
            states = [a * h + signal for a, h in zip(decay, states)]
            parts = [w * h for w, h in zip(weight, states)]
            parts.append(skip * signal)
            conv_ref[step] = added(parts)
        return (q2, q1, *states)

    first = (row(-2), row(-1), *[start_ref[r] for r in range(order)])
    lax.fori_loop(0, steps // UNROLL, body, first)


def gate_kernel(
    taps_ref, residue_ref, rate_ref, skip_ref, query_ref, conv_ref, own_ref, *rest
):
    *past_refs, out_ref, nat_ref = rest
    rows, chans = out_ref.shape
    steps = rows // SUB
    order = rate_ref.shape[0]
    rate = rate_ref[...]
    decay = jnp.exp(-rate)
    weight = residue_ref[...] * jnp.sqrt(2.0 * rate)
    tap = [[taps_ref[j, s : s + 1, :] for s in range(3)] for j in range(3)]

    def head_feat(now_ref, past_ref, s):
        at = order + 2 * s
        x0, x1 = now_ref[at : at + 1, :], now_ref[at + 1 : at + 2, :]
        at = order + 6 + 2 * s
        if past_ref is None:
            m2 = m1 = jnp.zeros_like(x0)
        else:
            m2, m1 = past_ref[at : at + 1, :], past_ref[at + 1 : at + 2, :]
        first = tap[0][s] * m2 + tap[1][s] * m1 + tap[2][s] * x0
        second = tap[0][s] * m1 + tap[1][s] * x0 + tap[2][s] * x1
        return first, second

    refs = [own_ref, *past_refs, None]

    def head_signal(at):
        k0, k1 = head_feat(refs[at], refs[at + 1], 1)
        v0, v1 = head_feat(refs[at], refs[at + 1], 2)
        return k0 * v0, k1 * v1

    whole = jnp.exp(-rate * rows)
    lead0 = jnp.exp(-rate * (rows - 1))
    lead1 = jnp.exp(-rate * (rows - 2))
    state = jnp.zeros((order, chans), jnp.float32)
    for at in range(len(past_refs), 0, -1):
        s0, s1 = head_signal(at)
        state = whole * state + refs[at][0:order, :] + lead0 * s0 + lead1 * s1
    s0, s1 = head_signal(0)
    at0 = decay * state + s0
    at1 = decay * at0 + s1
    skip = skip_ref[0:1, :]
    conv0 = jnp.sum(weight * at0, axis=0, keepdims=True) + skip * s0
    conv1 = jnp.sum(weight * at1, axis=0, keepdims=True) + skip * s1
    q0, q1 = head_feat(refs[0], refs[1], 0)

    block = lax.broadcasted_iota(jnp.int32, (SUB, chans), 0).astype(jnp.float32)
    begin = weight * at1
    decays = [wide(decay[r : r + 1, :]) for r in range(order)]
    terms = [
        wide(begin[r : r + 1, :]) * jnp.exp(-wide(rate[r : r + 1, :]) * (block * steps - 1.0))
        for r in range(order)
    ]

    def body(at, terms):
        for inner in range(UNROLL):
            step = at * UNROLL + inner
            parts = [conv_ref[step], *terms]
            nat_ref[pl.ds(step, SUB, stride=steps), :] = query_ref[step] * added(parts)
            terms = [p * a for p, a in zip(terms, decays)]
        return tuple(terms)

    lax.fori_loop(0, steps // UNROLL, body, tuple(terms))
    nat_ref[0:1, :] = q0 * conv0
    nat_ref[1:2, :] = q1 * conv1
    tile = 256

    def finish(at, _):
        span = pl.ds(pl.multiple_of(at * tile, tile), tile)
        out_ref[span, :] = nat_ref[span, :].astype(jnp.bfloat16)
        return 0

    lax.fori_loop(0, rows // tile, finish, 0)


def project_kernel(place_ref, *refs):
    here, f1, f2, f3, b1, b2, b3, f4, b4, w0, w1, w2, w3, own, p1, p2, p3, weight = refs
    rows = here.shape[0]
    count = w0.shape[0]
    depth = w0.shape[1]
    place = place_ref[0]
    for j in range(count):
        source = lax.rem(place - j + count, count)
        for s, piece in enumerate((w0, w1, w2, w3)):
            weight[j * depth : (j + 1) * depth, s * depth : (s + 1) * depth] = piece[source]
    for start in range(0, rows, ROW_TILE):
        span = slice(start, start + ROW_TILE)
        half = rows // 2
        far = f4[start : start + ROW_TILE, :] if start < half else b4[start - half : start - half + ROW_TILE, :]
        left = jnp.concatenate(
            [here[span, :], f1[span, :], f2[span, :], f3[span, :], far, b3[span, :], b2[span, :], b1[span, :]],
            axis=1,
        )
        total = jnp.dot(left, weight[...], preferred_element_type=jnp.float32)
        own[span, :] = total[:, 0:depth]
        for s, part in enumerate((p1, p2, p3)):
            part[span, :] = total[:, (s + 1) * depth : (s + 2) * depth].astype(jnp.bfloat16)


def call(kernel, shapes, scratch, flops, args, name):
    size = sum(a.size * a.dtype.itemsize for a in args) + sum(
        s.size * jnp.dtype(s.dtype).itemsize for s in jax.tree.leaves(shapes)
    )
    return pl.pallas_call(
        kernel,
        out_shape=shapes,
        scratch_shapes=scratch,
        compiler_params=pltpu.CompilerParams(vmem_limit_bytes=40 * 1024 * 1024),
        cost_estimate=pl.CostEstimate(flops=flops, bytes_accessed=size, transcendentals=0),
        name=name,
    )(*args)


def shards(streams, short_filter, residue, decay_rate, skip_gain, out_weight):
    f32, bf16 = jnp.float32, jnp.bfloat16
    rows, _, chans = streams.shape
    order = residue.shape[0]
    steps = rows // SUB
    z_size, y_size = lax.axis_size("z"), lax.axis_size("y")
    z_at, y_at = lax.axis_index("z"), lax.axis_index("y")
    shape = jax.ShapeDtypeStruct
    skip = skip_gain[None, :]

    by_owner = out_weight.reshape(z_size, y_size, chans, chans)
    weights = []
    for s in range(y_size):
        rows_of = lax.dynamic_index_in_dim(by_owner, (y_at + s) % y_size, 1, keepdims=False)
        weights.append(rows_of if s == 0 else shifted(rows_of, "y", s))

    planes = jnp.transpose(streams, (1, 0, 2))
    plane = pltpu.VMEM((PAD + rows, chans), f32)
    by_step = shape((steps, SUB, chans), f32)
    signal, start, packed = call(
        state_kernel,
        (by_step, shape((order, SUB, chans), f32), shape((order + 16, chans), f32)),
        [plane, plane],
        rows * chans * 44,
        (planes, short_filter, decay_rate),
        "states",
    )
    past = [from_behind(packed, CTX, s) for s in range(1, 8)]
    query, conv = call(
        local_kernel,
        (by_step, by_step),
        [plane],
        rows * chans * 70,
        (planes, short_filter, residue, decay_rate, skip, signal, start),
        "local_conv",
    )
    gated = call(
        gate_kernel,
        shape((rows, chans), bf16),
        [pltpu.VMEM((rows, chans), f32)],
        rows * chans * 34,
        (short_filter, residue, decay_rate, skip, query, conv, packed, *past),
        "gate",
    )

    place = z_at.astype(jnp.int32).reshape(1)
    count = rows // PIECES
    results = []
    for piece in range(PIECES):
        here = gated[piece * count : (piece + 1) * count]
        ahead, behind = [here], [here]
        for _ in range(3):
            ahead.append(shifted(ahead[-1], "z", 1))
            behind.append(shifted(behind[-1], "z", -1))
        f4 = shifted(ahead[3][: count // 2], "z", 1)
        b4 = shifted(behind[3][count // 2 :], "z", -1)
        part = shape((count, chans), bf16)
        smem = pl.BlockSpec(memory_space=pltpu.SMEM)
        vmem = pl.BlockSpec(memory_space=pltpu.VMEM)
        own, *parts = pl.pallas_call(
            project_kernel,
            out_shape=(shape((count, chans), f32), part, part, part),
            in_specs=[smem] + [vmem] * 13,
            out_specs=(vmem,) * 4,
            scratch_shapes=[pltpu.VMEM((z_size * chans, y_size * chans), bf16)],
            compiler_params=pltpu.CompilerParams(vmem_limit_bytes=40 * 1024 * 1024),
            cost_estimate=pl.CostEstimate(
                flops=2 * count * z_size * y_size * chans * chans,
                bytes_accessed=16 * count * chans * 2,
                transcendentals=0,
            ),
            name="project",
        )(place, *ahead, *behind[1:], f4, b4, *weights)
        total = own
        for s in range(1, y_size):
            total = total + shifted(parts[s - 1], "y", -s).astype(f32)
        results.append(total.astype(bf16))
    return jnp.concatenate(results, axis=0)


def solution(mesh):
    ctx_size, tp_size = mesh.devices.shape
    fine = Mesh(mesh.devices.reshape(ctx_size // 2, 2, tp_size // 4, 4), ("x", "core", "z", "y"))
    tp = ("z", "y")
    in_specs = (
        P(CTX, None, tp),
        P(None, None, tp),
        P(None, tp),
        P(None, tp),
        P(tp),
        P(None, tp),
    )
    return jax.shard_map(shards, mesh=fine, in_specs=in_specs, out_specs=P(CTX, tp), check_vma=False)
```

```python
import jax
import jax.numpy as jnp
from jax import lax
from jax.experimental import pallas as pl
from jax.experimental.pallas import tpu as pltpu
from jax.sharding import Mesh, PartitionSpec as P

CTX = ("x", "core")
SUB = 8
PAD = 8
UNROLL = 8
PIECES = (1024, 1024)
VMEM_LIMIT = 16 * 1024 * 1024
ROW_TILE = 256


def shifted(value, axis, steps):
    count = lax.axis_size(axis)
    return lax.ppermute(value, axis, [(at, (at + steps) % count) for at in range(count)])


def from_behind(value, axis, steps):
    count = lax.axis_size(axis)
    return lax.ppermute(value, axis, [(at, at + steps) for at in range(count - steps)])


def wide(row):
    return jnp.broadcast_to(row, (SUB, row.shape[-1]))


def added(parts):
    while len(parts) > 1:
        pairs = [a + b for a, b in zip(parts[0::2], parts[1::2])]
        parts = pairs + parts[2 * len(pairs) :]
    return parts[0]


def unpack_stream(raw_ref, padded_ref, first=0, last=None):
    last = raw_ref.shape[0] if last is None else last
    if first == 0:
        padded_ref[0:PAD, :] = jnp.zeros((PAD, padded_ref.shape[1]), jnp.float32)
    tile = 128
    for at in range(first, last, tile):
        padded_ref[PAD + at : PAD + at + tile, :] = raw_ref[at : at + tile, :].astype(jnp.float32)


def mode_rows(taps_ref, rate_ref, residue_ref):
    taps = lambda j, s: taps_ref[j, s : s + 1, :]
    rate = rate_ref[...]
    return taps, rate, residue_ref[...] * jnp.sqrt(2.0 * rate)


def state_kernel(stream_ref, taps_ref, rate_ref, signal_ref, start_ref, packed_ref, key_ref, val_ref):
    rows = stream_ref.shape[1]
    steps = rows // SUB
    order, _, chans = start_ref.shape
    unpack_stream(stream_ref.at[1], key_ref)
    unpack_stream(stream_ref.at[2], val_ref)
    taps, rates, _ = mode_rows(taps_ref, rate_ref, rate_ref)
    fade = jnp.exp(-rates)
    decay = [wide(fade[r : r + 1, :]) for r in range(order)]
    key_taps = [wide(taps(j, 1)) for j in range(3)]
    val_taps = [wide(taps(j, 2)) for j in range(3)]
    block = lax.broadcasted_iota(jnp.int32, (SUB, chans), 0)

    def row(ref, step):
        return ref[pl.ds(PAD + step, SUB, stride=steps), :]

    def advance(step, carried, masked):
        k2, k1, v2, v1, *states = carried
        k0 = row(key_ref, step)
        v0 = row(val_ref, step)
        key = key_taps[0] * k2 + key_taps[1] * k1 + key_taps[2] * k0
        val = val_taps[0] * v2 + val_taps[1] * v1 + val_taps[2] * v0
        signal = key * val
        if masked:
            signal = jnp.where(block == 0, 0.0, signal)
        signal_ref[step] = signal
        states = [a * h + signal for a, h in zip(decay, states)]
        return [k1, k0, v1, v0, *states]

    carried = [row(key_ref, -2), row(key_ref, -1), row(val_ref, -2), row(val_ref, -1)]
    carried += [jnp.zeros((SUB, chans), jnp.float32)] * order
    for step in range(UNROLL):
        carried = advance(step, carried, step < 2)

    def body(at, carried):
        carried = list(carried)
        for step in range(UNROLL):
            carried = advance(at * UNROLL + step, carried, False)
        return tuple(carried)

    states = lax.fori_loop(1, steps // UNROLL, body, tuple(carried))[4:]
    for r in range(order):
        rate = wide(rates[r : r + 1, :])
        total = states[r]
        for back in (1, 2, 4):
            gain = jnp.where(block >= back, jnp.exp(-rate * (steps * back)), 0.0)
            total = total + gain * pltpu.roll(total, back, 0)
        packed_ref[r : r + 1, :] = total[SUB - 1 : SUB, :]
        start_ref[r] = jnp.where(block == 0, 0.0, pltpu.roll(total, 1, 0))
    heads = [
        stream_ref[0, 0:16, :].astype(jnp.float32)[0:2, :],
        key_ref[PAD : PAD + 2, :],
        val_ref[PAD : PAD + 2, :],
    ]
    tails = [
        stream_ref[0, rows - 16 : rows, :].astype(jnp.float32)[14:16, :],
        key_ref[PAD + rows - 2 : PAD + rows, :],
        val_ref[PAD + rows - 2 : PAD + rows, :],
    ]
    for s in range(3):
        packed_ref[order + 2 * s : order + 2 * s + 2, :] = heads[s]
        packed_ref[order + 6 + 2 * s : order + 8 + 2 * s, :] = tails[s]
    packed_ref[order + 12 :, :] = jnp.zeros((packed_ref.shape[0] - order - 12, chans), jnp.float32)


def local_kernel(
    stream_ref, taps_ref, rate_ref, residue_ref, skip_ref, signal_ref, start_ref, query_ref, conv_ref, raw_ref
):
    rows = stream_ref.shape[1]
    steps = rows // SUB
    order = start_ref.shape[0]
    unpack_stream(stream_ref.at[0], raw_ref)
    taps, rate, weights = mode_rows(taps_ref, rate_ref, residue_ref)
    fade = jnp.exp(-rate)
    decay = [wide(fade[r : r + 1, :]) for r in range(order)]
    weight = [wide(weights[r : r + 1, :]) for r in range(order)]
    taps = [wide(taps(j, 0)) for j in range(3)]
    skip = wide(skip_ref[0:1, :])

    def row(step):
        return raw_ref[pl.ds(PAD + step, SUB, stride=steps), :]

    def body(at, carried):
        q2, q1, *states = carried
        for inner in range(UNROLL):
            step = at * UNROLL + inner
            q0 = row(step)
            query_ref[step] = taps[0] * q2 + taps[1] * q1 + taps[2] * q0
            q2, q1 = q1, q0
            signal = signal_ref[step]
            states = [a * h + signal for a, h in zip(decay, states)]
            parts = [w * h for w, h in zip(weight, states)]
            parts.append(skip * signal)
            conv_ref[step] = added(parts)
        return (q2, q1, *states)

    carried = (row(-2), row(-1), *[start_ref[r] for r in range(order)])
    lax.fori_loop(0, steps // UNROLL, body, carried)


def pack_kernel(*refs):
    *parts, out_ref = refs
    for at, part in enumerate(parts):
        out_ref[at] = part[...]


def gate_kernel(core_ref, taps_ref, rate_ref, residue_ref, skip_ref, query_ref, conv_ref, *rest):
    *own_refs, other_ref, out_ref, nat_ref, ends_ref = rest
    rows, chans = out_ref.shape
    steps = rows // SUB
    core = core_ref[0]
    for back, own_ref in enumerate(own_refs):
        pair = 2 * (len(own_refs) - 1 - back)
        ends_ref[pair + core] = own_ref[...]
        ends_ref[pair + 1 - core] = other_ref[back]
    taps, rate, weight = mode_rows(taps_ref, rate_ref, residue_ref)
    skip = skip_ref[0:1, :]
    order = rate.shape[0]
    decay = jnp.exp(-rate)
    tap = [[taps(j, s) for s in range(3)] for j in range(3)]

    def head_feat(at, s):
        head, tail = order + 2 * s, order + 6 + 2 * s
        x0, x1 = ends_ref[at, head : head + 1, :], ends_ref[at, head + 1 : head + 2, :]
        if isinstance(at, int) and at == 0:
            m2 = m1 = jnp.zeros_like(x0)
        else:
            m2, m1 = ends_ref[at - 1, tail : tail + 1, :], ends_ref[at - 1, tail + 1 : tail + 2, :]
        first = tap[0][s] * m2 + tap[1][s] * m1 + tap[2][s] * x0
        second = tap[0][s] * m1 + tap[1][s] * x0 + tap[2][s] * x1
        return first, second

    whole = jnp.exp(-rate * rows)
    lead0 = jnp.exp(-rate * (rows - 1))
    lead1 = jnp.exp(-rate * (rows - 2))
    running = jnp.zeros((order, chans), jnp.float32)
    last = ends_ref.shape[0]
    for at in range(last):
        k0, k1 = head_feat(at, 1)
        v0, v1 = head_feat(at, 2)
        h0, h1 = head_feat(at, 0)
        now = (running, k0 * v0, k1 * v1, h0, h1)
        if at == last - 2:
            state, s0, s1, q0, q1 = now
        elif at == last - 1:
            state, s0, s1, q0, q1 = [
                jnp.where(core == 1, new, old) for new, old in zip(now, (state, s0, s1, q0, q1))
            ]
        running = whole * running + ends_ref[at, 0:order, :] + lead0 * now[1] + lead1 * now[2]
    at0 = decay * state + s0
    at1 = decay * at0 + s1
    conv0 = jnp.sum(weight * at0, axis=0, keepdims=True) + skip * s0
    conv1 = jnp.sum(weight * at1, axis=0, keepdims=True) + skip * s1

    block = lax.broadcasted_iota(jnp.int32, (SUB, chans), 0).astype(jnp.float32)
    begin = weight * at1
    decays = [wide(decay[r : r + 1, :]) for r in range(order)]
    terms = [
        wide(begin[r : r + 1, :]) * jnp.exp(-wide(rate[r : r + 1, :]) * (block * steps - 1.0))
        for r in range(order)
    ]

    def body(at, terms):
        for inner in range(UNROLL):
            step = at * UNROLL + inner
            nat_ref[pl.ds(step, SUB, stride=steps), :] = query_ref[step] * added([conv_ref[step], *terms])
            terms = [p * a for p, a in zip(terms, decays)]
        return tuple(terms)

    lax.fori_loop(0, steps // UNROLL, body, tuple(terms))
    nat_ref[0:1, :] = q0 * conv0
    nat_ref[1:2, :] = q1 * conv1
    tile = 128
    for at in range(0, rows, tile):
        out_ref[at : at + tile, :] = nat_ref[at : at + tile, :].astype(jnp.bfloat16)


def pick_kernel(turn_ref, by_owner_ref, *out_refs):
    count = by_owner_ref.shape[1]
    for s, out_ref in enumerate(out_refs):
        out_ref[...] = by_owner_ref[:, lax.rem(turn_ref[0] + s + 1, count)]


def weight_kernel(turn_ref, by_owner_ref, *refs):
    *pieces, weight = refs
    count, _, depth, _ = by_owner_ref.shape
    for j in range(count):
        source = lax.rem(turn_ref[1] - j + count, count)
        rows = slice(j * depth, (j + 1) * depth)
        weight[rows, 0:depth] = by_owner_ref[source, turn_ref[0]]
        for s, piece in enumerate(pieces):
            weight[rows, (s + 1) * depth : (s + 2) * depth] = piece[source]


def project_kernel(here, f1, f2, f3, b1, b2, b3, far, weight, own, p1, p2, p3):
    rows, depth = here.shape
    for start in range(0, rows, ROW_TILE):
        span = slice(start, start + ROW_TILE)
        order = (here, f1, f2, f3, far, b3, b2, b1)
        left = jnp.concatenate([piece[span, :] for piece in order], axis=1)
        total = jnp.dot(left, weight[...], preferred_element_type=jnp.float32)
        own[span, :] = total[:, 0:depth]
        for s, part in enumerate((p1, p2, p3)):
            part[span, :] = total[:, (s + 1) * depth : (s + 2) * depth].astype(jnp.bfloat16)


def call(kernel, shapes, scratch, flops, args, name, limit=VMEM_LIMIT, **more):
    size = sum(a.size * a.dtype.itemsize for a in args) + sum(
        s.size * jnp.dtype(s.dtype).itemsize for s in jax.tree.leaves(shapes)
    )
    return pl.pallas_call(
        kernel,
        out_shape=shapes,
        scratch_shapes=scratch,
        compiler_params=pltpu.CompilerParams(vmem_limit_bytes=limit),
        cost_estimate=pl.CostEstimate(flops=flops, bytes_accessed=size, transcendentals=0),
        name=name,
        **more,
    )(*args)


def shards(streams, short_filter, residue, decay_rate, skip_gain, out_weight):
    f32, bf16 = jnp.float32, jnp.bfloat16
    rows, _, chans = streams.shape
    order = residue.shape[0]
    steps = rows // SUB
    z_size, y_size = lax.axis_size("z"), lax.axis_size("y")
    z_at, y_at = lax.axis_index("z"), lax.axis_index("y")
    shape = jax.ShapeDtypeStruct

    smem = pl.BlockSpec(memory_space=pltpu.SMEM)
    vmem = pl.BlockSpec(memory_space=pltpu.VMEM)
    planes = jnp.transpose(streams, (1, 0, 2))
    plane = pltpu.VMEM((PAD + rows, chans), f32)
    by_step = shape((steps, SUB, chans), f32)
    modes = (short_filter, decay_rate, residue, skip_gain[None, :])
    signal, start, packed = call(
        state_kernel,
        (by_step, shape((order, SUB, chans), f32), shape((order + 16, chans), f32)),
        [plane, plane],
        rows * chans * 44,
        (planes, short_filter, decay_rate),
        "states",
    )
    own_ends = [packed] + [from_behind(packed, "x", s) for s in range(1, lax.axis_size("x"))]
    feat, conv = call(
        local_kernel,
        (by_step, by_step),
        [plane],
        rows * chans * 70,
        (planes, *modes, signal, start),
        "local_conv",
    )
    own_ends, conv = lax.optimization_barrier((own_ends, conv))
    ends = call(
        pack_kernel, shape((len(own_ends), *packed.shape), f32), [], 8 * packed.size, own_ends, "pack"
    )
    other_ends = shifted(ends, "core", 1)
    gated = call(
        gate_kernel,
        shape((rows, chans), bf16),
        [pltpu.VMEM((rows, chans), f32), pltpu.VMEM((2 * len(own_ends), *packed.shape), f32)],
        rows * chans * 34,
        (
            lax.axis_index("core").astype(jnp.int32).reshape(1),
            *modes,
            feat,
            conv,
            *own_ends,
            other_ends,
        ),
        "gate",
        in_specs=[smem] + [vmem] * (7 + len(own_ends)),
        out_specs=vmem,
    )

    bounds = [0]
    for count in PIECES:
        bounds.append(bounds[-1] + count)
    here = [gated[lo:hi] for lo, hi in zip(bounds, bounds[1:])]
    ahead, behind = [[h] for h in here], [[h] for h in here]

    def after(value, *others):
        return lax.optimization_barrier((value, *others))[0]

    def hop(piece, number):
        if number < 3 or piece == 0:
            ahead[piece].append(shifted(ahead[piece][-1], "z", 1))
        if number < 3 or piece == 1:
            behind[piece].append(shifted(behind[piece][-1], "z", -1))

    for number in range(4):
        hop(0, number)
        hop(1, number)
    turn = jnp.stack([y_at, z_at]).astype(jnp.int32)
    by_owner = out_weight.reshape(z_size, y_size, chans, chans)
    block = shape((z_size, chans, chans), bf16)
    sources = call(
        pick_kernel,
        (block,) * (y_size - 1),
        [],
        out_weight.size,
        (turn, after(by_owner, gated)),
        "pick",
        in_specs=[smem, vmem],
        out_specs=(vmem,) * (y_size - 1),
    )
    ties = (ahead[0][1], ahead[0][2], ahead[1][2])
    weights = [shifted(after(w, tie), "y", s + 1) for s, (w, tie) in enumerate(zip(sources, ties))]
    weight = call(
        weight_kernel,
        shape((z_size * chans, y_size * chans), bf16),
        [],
        out_weight.size,
        (turn, by_owner, *weights),
        "weights",
        in_specs=[smem] + [vmem] * y_size,
        out_specs=vmem,
    )
    ahead[0][0] = after(ahead[0][0], behind[1][3])

    def project(piece):
        count = PIECES[piece]
        part = shape((count, chans), bf16)
        own, *parts = call(
            project_kernel,
            (shape((count, chans), f32), part, part, part),
            [],
            2 * count * z_size * y_size * chans * chans,
            (*ahead[piece][:4], *behind[piece][1:4], (ahead, behind)[piece][piece][4], weight),
            "project",
        )
        total = own
        for s in range(1, y_size):
            total = total + shifted(parts[s - 1], "y", -s).astype(f32)
        return total.astype(bf16)

    return jnp.concatenate([project(piece) for piece in range(len(PIECES))], axis=0)


def solution(mesh):
    ctx_size, tp_size = mesh.devices.shape
    fine = Mesh(mesh.devices.reshape(ctx_size // 2, 2, tp_size // 4, 4), ("x", "core", "z", "y"))
    tp = ("z", "y")
    in_specs = (
        P(CTX, None, tp),
        P(None, None, tp),
        P(None, tp),
        P(None, tp),
        P(tp),
        P(None, tp),
    )
    return jax.shard_map(shards, mesh=fine, in_specs=in_specs, out_specs=P(CTX, tp), check_vma=False)
```

```python
import math

import jax
import jax.numpy as jnp
from jax import lax
from jax.experimental import pallas as pl
from jax.experimental.pallas import tpu as pltpu
from jax.sharding import Mesh, PartitionSpec as P

CTX = ("x", "core")
SUB = 8
PAD = 8
UNROLL = 8
HALF = 1024
KINDS = (2, 1, 3)
LOADS = 4
BACK = (0, 2, 1, 3)
VMEM_LIMIT = 16 * 1024 * 1024
ROW_TILE = 256


def shifted(value, axis, steps):
    count = lax.axis_size(axis)
    return lax.ppermute(value, axis, [(at, (at + steps) % count) for at in range(count)])


def swapped(value, kind):
    count = lax.axis_size("y")
    pairs = []
    for core in range(2):
        flip = kind if kind == 2 or core == 0 else 4 - kind
        pairs += [(core * count + at, core * count + (at ^ flip)) for at in range(count)]
    return lax.ppermute(value, ("core", "y"), pairs)


def peers():
    core, here = lax.axis_index("core"), lax.axis_index("y")
    return {kind: here ^ (kind + core * (4 - 2 * kind)) for kind in (1, 2, 3)}


def from_behind(value, axis, steps):
    count = lax.axis_size(axis)
    return lax.ppermute(value, axis, [(at, at + steps) for at in range(count - steps)])


def wide(row):
    return jnp.broadcast_to(row, (SUB, row.shape[-1]))


def added(parts):
    while len(parts) > 1:
        pairs = [a + b for a, b in zip(parts[0::2], parts[1::2])]
        parts = pairs + parts[2 * len(pairs) :]
    return parts[0]


def widen(raw, padded_ref, first, last):
    blocks, steps, _ = raw.shape
    for c in range(blocks):
        at = c * (steps + PAD) + PAD
        padded_ref[at + first : at + last, :] = raw[c, first:last, :].astype(jnp.float32)


def lead_in(tails, padded_ref, steps):
    blocks, count, chans = tails.shape
    padded_ref[PAD - 2 : PAD, :] = jnp.zeros((2, chans), jnp.float32)
    for c in range(1, blocks):
        at = c * (steps + PAD) + PAD
        padded_ref[at - 2 : at, :] = tails[c - 1].astype(jnp.float32)[count - 2 : count, :]


def row_of(ref, step, steps):
    return ref[pl.ds(PAD + step, SUB, stride=steps + PAD), :]


def mode_rows(param_ref):
    order = (param_ref.shape[0] - 16) // 3
    taps = lambda j, s: param_ref[3 * j + s : 3 * j + s + 1, :]
    rate, decay, weight = [param_ref[16 + order * i : 16 + order * (i + 1), :] for i in range(3)]
    return taps, param_ref[9:10, :], rate, decay, weight


def state_kernel(stream_hbm, taps_hbm, rate_hbm, residue_hbm, skip_hbm, *rest):
    signal_ref, start_ref, packed_ref, param_ref, *scratch = rest
    raw_ref, tail_ref, edge_ref, taps_ref, rate_ref, residue_ref, skip_ref, key_ref, val_ref, sems = scratch
    _, blocks, steps, chans = stream_hbm.shape
    order = rate_ref.shape[0]
    pair = pl.ds(1, 2)
    part = steps // LOADS
    sources = [
        (stream_hbm.at[pair, :, pl.ds(steps - 16, 16)], tail_ref),
        (taps_hbm, taps_ref),
        (rate_hbm, rate_ref),
        (residue_hbm, residue_ref),
        (skip_hbm, skip_ref),
        (stream_hbm.at[0, 0, pl.ds(0, 16)], edge_ref.at[0]),
        (stream_hbm.at[0, blocks - 1, pl.ds(steps - 16, 16)], edge_ref.at[1]),
    ]
    for at in range(LOADS):
        span = pl.ds(at * part, part)
        sources.append((stream_hbm.at[pair, :, span], raw_ref.at[:, :, span]))
    copies = [pltpu.make_async_copy(*pair, sems.at[i]) for i, pair in enumerate(sources)]
    small, large = copies[:-LOADS], copies[-LOADS:]
    for copy in small[:3] + large + small[3:]:
        copy.start()
    for copy in small:
        copy.wait()

    for j in range(3):
        for s in range(3):
            param_ref[3 * j + s : 3 * j + s + 1, :] = taps_ref[j, s : s + 1, :]
    param_ref[9:10, :] = skip_ref[...]
    param_ref[10:16, :] = jnp.zeros((6, chans), jnp.float32)
    rates = rate_ref[...]
    param_ref[16 : 16 + order, :] = rates
    param_ref[16 + order : 16 + 2 * order, :] = jnp.exp(-rates)
    param_ref[16 + 2 * order : 16 + 3 * order, :] = residue_ref[...] * jnp.sqrt(2.0 * rates)
    taps, _, _, fade, _ = mode_rows(param_ref)
    lead_in(tail_ref.at[0], key_ref, steps)
    lead_in(tail_ref.at[1], val_ref, steps)

    decay = [wide(fade[r : r + 1, :]) for r in range(order)]
    key_taps = [wide(taps(j, 1)) for j in range(3)]
    val_taps = [wide(taps(j, 2)) for j in range(3)]
    block = lax.broadcasted_iota(jnp.int32, (SUB, chans), 0)

    def advance(step, carried, masked):
        k2, k1, v2, v1, *states = carried
        k0 = row_of(key_ref, step, steps)
        v0 = row_of(val_ref, step, steps)
        key = key_taps[0] * k2 + key_taps[1] * k1 + key_taps[2] * k0
        val = val_taps[0] * v2 + val_taps[1] * v1 + val_taps[2] * v0
        signal = key * val
        if masked:
            signal = jnp.where(block == 0, 0.0, signal)
        signal_ref[step] = signal
        states = [a * h + signal for a, h in zip(decay, states)]
        return [k1, k0, v1, v0, *states]

    def body(at, carried):
        carried = list(carried)
        for step in range(UNROLL):
            carried = advance(at * UNROLL + step, carried, False)
        return tuple(carried)

    carried = [row_of(ref, step, steps) for ref in (key_ref, val_ref) for step in (-2, -1)]
    carried += [jnp.zeros((SUB, chans), jnp.float32)] * order
    for at in range(LOADS):
        large[at].wait()
        for which, ref in enumerate((key_ref, val_ref)):
            widen(raw_ref.at[which], ref, at * part, (at + 1) * part)
        begin = at * part // UNROLL
        if at == 0:
            for step in range(UNROLL):
                carried = advance(step, carried, step < 2)
            begin = 1
        carried = lax.fori_loop(begin, (at + 1) * part // UNROLL, body, tuple(carried))
    states = carried[4:]
    for r in range(order):
        rate = wide(rates[r : r + 1, :])
        total = states[r]
        for back in (1, 2, 4):
            gain = jnp.where(block >= back, jnp.exp(-rate * (steps * back)), 0.0)
            total = total + gain * pltpu.roll(total, back, 0)
        packed_ref[r : r + 1, :] = total[SUB - 1 : SUB, :]
        start_ref[r] = jnp.where(block == 0, 0.0, pltpu.roll(total, 1, 0))
    end = blocks * (steps + PAD)
    heads = [edge_ref[0].astype(jnp.float32)[0:2, :], key_ref[PAD : PAD + 2, :], val_ref[PAD : PAD + 2, :]]
    tails = [
        edge_ref[1].astype(jnp.float32)[14:16, :],
        key_ref[end - 2 : end, :],
        val_ref[end - 2 : end, :],
    ]
    for s in range(3):
        packed_ref[order + 2 * s : order + 2 * s + 2, :] = heads[s]
        packed_ref[order + 6 + 2 * s : order + 8 + 2 * s, :] = tails[s]
    packed_ref[order + 12 :, :] = jnp.zeros((packed_ref.shape[0] - order - 12, chans), jnp.float32)


def local_steps(first, param_ref, signal_ref, start_ref, conv_ref):
    order = start_ref.shape[0]
    _, skip, _, decay, weight = mode_rows(param_ref)
    decay = [wide(decay[r : r + 1, :]) for r in range(order)]
    weight = [wide(weight[r : r + 1, :]) for r in range(order)]
    skip = wide(skip)

    def body(at, states):
        for inner in range(UNROLL):
            step = at * UNROLL + inner
            signal = signal_ref[first + step]
            states = [a * h + signal for a, h in zip(decay, states)]
            conv_ref[step] = added([w * h for w, h in zip(weight, states)] + [skip * signal])
        return tuple(states)

    states = tuple(start_ref[r] for r in range(order))
    return lax.fori_loop(0, conv_ref.shape[0] // UNROLL, body, states)


def local_kernel(param_ref, signal_ref, start_ref, conv_ref, next_ref):
    states = local_steps(0, param_ref, signal_ref, start_ref, conv_ref)
    for r, state in enumerate(states):
        next_ref[r] = state


def local_query_kernel(stream_hbm, param_ref, signal_ref, start_ref, conv_ref, query_ref, raw_ref, wide_ref, sem):
    copy = pltpu.make_async_copy(stream_hbm.at[0], raw_ref, sem)
    copy.start()
    blocks, steps, _ = raw_ref.shape
    local_steps(conv_ref.shape[0], param_ref, signal_ref, start_ref, conv_ref)
    copy.wait()
    widen(raw_ref, wide_ref, 0, steps)
    lead_in(raw_ref.at[:, pl.ds(steps - 16, 16)], wide_ref, steps)
    taps = [wide(mode_rows(param_ref)[0](j, 0)) for j in range(3)]

    def body(at, carried):
        q2, q1 = carried
        for inner in range(UNROLL):
            step = at * UNROLL + inner
            q0 = row_of(wide_ref, step, steps)
            query_ref[step] = taps[0] * q2 + taps[1] * q1 + taps[2] * q0
            q2, q1 = q1, q0
        return q2, q1

    lax.fori_loop(0, steps // UNROLL, body, (row_of(wide_ref, -2, steps), row_of(wide_ref, -1, steps)))


def pack_kernel(*refs):
    *parts, out_ref = refs
    at = 0
    for part in parts:
        count = 1 if len(part.shape) == 2 else part.shape[0]
        out_ref[at : at + count] = part[...].reshape(count, *out_ref.shape[1:])
        at += count


def gate_kernel(param_ref, query_ref, conv0_ref, conv1_ref, *rest):
    *own_refs, other_ref, out_ref, nat_ref, ends_ref = rest
    rows, chans = out_ref.shape
    steps = rows // SUB
    core = lax.axis_index("core")
    for at, (back, own_ref) in enumerate(zip(BACK, own_refs)):
        pair = 2 * (len(own_refs) - 1 - back)
        ends_ref[pair + core] = own_ref[...]
        ends_ref[pair + 1 - core] = other_ref[at]
    taps, skip, rate, decay, weight = mode_rows(param_ref)
    order = rate.shape[0]
    tap = [[taps(j, s) for s in range(3)] for j in range(3)]

    def head_feat(at, s):
        head, tail = order + 2 * s, order + 6 + 2 * s
        x0, x1 = ends_ref[at, head : head + 1, :], ends_ref[at, head + 1 : head + 2, :]
        if isinstance(at, int) and at == 0:
            m2 = m1 = jnp.zeros_like(x0)
        else:
            m2, m1 = ends_ref[at - 1, tail : tail + 1, :], ends_ref[at - 1, tail + 1 : tail + 2, :]
        first = tap[0][s] * m2 + tap[1][s] * m1 + tap[2][s] * x0
        second = tap[0][s] * m1 + tap[1][s] * x0 + tap[2][s] * x1
        return first, second

    whole = jnp.exp(-rate * rows)
    lead0 = jnp.exp(-rate * (rows - 1))
    lead1 = jnp.exp(-rate * (rows - 2))
    running = jnp.zeros((order, chans), jnp.float32)
    last = ends_ref.shape[0]
    for at in range(last):
        k0, k1 = head_feat(at, 1)
        v0, v1 = head_feat(at, 2)
        h0, h1 = head_feat(at, 0)
        now = (running, k0 * v0, k1 * v1, h0, h1)
        if at == last - 2:
            state, s0, s1, q0, q1 = now
        elif at == last - 1:
            state, s0, s1, q0, q1 = [
                jnp.where(core == 1, new, old) for new, old in zip(now, (state, s0, s1, q0, q1))
            ]
        running = whole * running + ends_ref[at, 0:order, :] + lead0 * now[1] + lead1 * now[2]
    at0 = decay * state + s0
    at1 = decay * at0 + s1
    conv0 = jnp.sum(weight * at0, axis=0, keepdims=True) + skip * s0
    conv1 = jnp.sum(weight * at1, axis=0, keepdims=True) + skip * s1

    block = lax.broadcasted_iota(jnp.int32, (SUB, chans), 0).astype(jnp.float32)
    begin = weight * at1
    decays = [wide(decay[r : r + 1, :]) for r in range(order)]
    terms = [
        wide(begin[r : r + 1, :]) * jnp.exp(-wide(rate[r : r + 1, :]) * (block * steps - 1.0))
        for r in range(order)
    ]

    terms = tuple(terms)
    for which, conv_ref in enumerate((conv0_ref, conv1_ref)):
        count = conv_ref.shape[0]

        def body(at, terms):
            for inner in range(UNROLL):
                local = at * UNROLL + inner
                step = which * count + local
                conv = added([conv_ref[local], *terms])
                nat_ref[pl.ds(step, SUB, stride=steps), :] = query_ref[step] * conv
                terms = [p * a for p, a in zip(terms, decays)]
            return tuple(terms)

        terms = lax.fori_loop(0, count // UNROLL, body, terms)
    nat_ref[0:1, :] = q0 * conv0
    nat_ref[1:2, :] = q1 * conv1
    tile = 128
    for at in range(0, rows, tile):
        out_ref[at : at + tile, :] = nat_ref[at : at + tile, :].astype(jnp.bfloat16)


def pick_kernel(by_owner_ref, near, far):
    peer = peers()
    count = far.shape[0]
    near[...] = by_owner_ref[:, peer[1]]
    far[...] = by_owner_ref[pl.ds(lax.axis_index("core") * count, count), peer[2]]


def weight_kernel(by_owner_ref, near, next_near, far, next_far, weight):
    count, _, depth, _ = by_owner_ref.shape
    half = far.shape[0]
    here, core = lax.axis_index("y"), lax.axis_index("core")
    for j in range(count):
        source = lax.rem(lax.axis_index("z") - j + count, count)
        within = lax.rem(source, half)
        mine = core * half <= source
        mine = mine & (source < core * half + half)
        far_block = jnp.where(mine, far[within], next_far[within])
        rows = slice(j * depth, (j + 1) * depth)
        for s, block in enumerate((by_owner_ref[source, here], far_block, near[source], next_near[source])):
            weight[rows, s * depth : (s + 1) * depth] = block


def project_kernel(here, f1, f2, f3, f4, b1, b2, b3, b4, weight, own, *sent):
    rows, depth = here.shape
    for start in range(0, rows, ROW_TILE):
        span = slice(start, start + ROW_TILE)
        near = [piece[span, :] for piece in (here, f1, f2, f3, b3, b2, b1)]
        half = rows // 2
        far = f4[span, :] if start < half else b4[start - half : start - half + ROW_TILE, :]
        left = jnp.concatenate([*near[:4], far, *near[4:]], axis=1)
        total = jnp.dot(left, weight[...], preferred_element_type=jnp.float32)
        own[span, :] = total[:, 0:depth]
        for s, part in enumerate(sent):
            part[span, :] = total[:, (s + 1) * depth : (s + 2) * depth].astype(jnp.bfloat16)


def finish_kernel(*refs):
    *parts, out = refs
    count = len(parts) // 2
    rows = parts[0].shape[0]
    tile = 128
    for piece in range(2):
        for at in range(0, rows, tile):
            total = parts[piece * count][at : at + tile, :]
            for part in parts[piece * count + 1 : (piece + 1) * count]:
                total = total + part[at : at + tile, :].astype(jnp.float32)
            out[piece * rows + at : piece * rows + at + tile, :] = total.astype(jnp.bfloat16)


def call(kernel, shapes, scratch, flops, args, name, limit=VMEM_LIMIT, **more):
    arrays = [*args, *jax.tree.leaves(shapes, is_leaf=lambda s: hasattr(s, "dtype"))]
    size = sum(math.prod(a.shape) * jnp.dtype(a.dtype).itemsize for a in arrays)
    return pl.pallas_call(
        kernel,
        out_shape=shapes,
        scratch_shapes=scratch,
        compiler_params=pltpu.CompilerParams(vmem_limit_bytes=limit),
        cost_estimate=pl.CostEstimate(flops=flops, bytes_accessed=size, transcendentals=0),
        name=name,
        **more,
    )(*args)


def shards(streams, short_filter, residue, decay_rate, skip_gain, out_weight):
    f32, bf16 = jnp.float32, jnp.bfloat16
    rows, _, chans = streams.shape
    order = residue.shape[0]
    steps = rows // SUB
    z_size, y_size = lax.axis_size("z"), lax.axis_size("y")
    shape = jax.ShapeDtypeStruct

    vmem = pl.BlockSpec(memory_space=pltpu.VMEM)
    def in_hbm(value):
        return pltpu.with_memory_space_constraint(value, pltpu.HBM)

    hbm = pl.BlockSpec(memory_space=pltpu.HBM)
    planes = in_hbm(jnp.transpose(streams, (1, 0, 2)).reshape(3, SUB, steps, chans))
    padded = pltpu.VMEM((SUB * (steps + PAD), chans), f32)
    modes = [in_hbm(m) for m in (short_filter, decay_rate, residue, skip_gain[None, :])]
    signal, start, packed, params = call(
        state_kernel,
        (
            pltpu.VMEM((steps, SUB, chans), f32),
            pltpu.VMEM((order, SUB, chans), f32),
            pltpu.VMEM((order + 16, chans), f32),
            pltpu.VMEM((16 + 3 * order, chans), f32),
        ),
        [
            pltpu.VMEM((2, SUB, steps, chans), bf16),
            pltpu.VMEM((2, SUB, 16, chans), bf16),
            pltpu.VMEM((2, 16, chans), bf16),
            *[pltpu.VMEM(m.shape, f32) for m in modes],
            padded,
            padded,
            pltpu.SemaphoreType.DMA((7 + LOADS,)),
        ],
        rows * chans * 44,
        (planes, *modes),
        "states",
        in_specs=[hbm] * 5,
        out_specs=(vmem,) * 4,
    )
    half_steps = pltpu.VMEM((steps // 2, SUB, chans), f32)
    past = {back: from_behind(packed, "x", back) for back in BACK[1:]}
    conv0, middle = call(
        local_kernel,
        (half_steps, pltpu.VMEM((order, SUB, chans), f32)),
        [],
        rows * chans * 33,
        (params, signal, start),
        "local_conv",
        in_specs=[vmem] * 3,
        out_specs=(vmem,) * 2,
    )
    conv1, query = call(
        local_query_kernel,
        (half_steps, pltpu.VMEM((steps, SUB, chans), f32)),
        [pltpu.VMEM((SUB, steps, chans), bf16), padded, pltpu.SemaphoreType.DMA],
        rows * chans * 40,
        (planes, params, signal, middle),
        "local_conv_query",
        in_specs=[hbm] + [vmem] * 3,
        out_specs=(vmem,) * 2,
    )
    own_ends, _ = lax.optimization_barrier(((packed, *[past[back] for back in BACK[1:]]), conv1))
    ends = call(
        pack_kernel, shape((len(own_ends), *packed.shape), f32), [], 4 * packed.size, own_ends, "pack"
    )
    other_ends = shifted(ends, "core", 1)
    gated = call(
        gate_kernel,
        shape((rows, chans), bf16),
        [pltpu.VMEM((rows, chans), f32), pltpu.VMEM((8, *packed.shape), f32)],
        rows * chans * 34,
        (params, query, conv0, conv1, *own_ends, other_ends),
        "gate",
        in_specs=[vmem] * 9,
        out_specs=vmem,
    )

    by_owner = out_weight.reshape(z_size, y_size, chans, chans)
    near, far = call(
        pick_kernel,
        (shape((z_size, chans, chans), bf16), shape((z_size // 2, chans, chans), bf16)),
        [],
        out_weight.size,
        (lax.optimization_barrier((by_owner, gated))[0],),
        "pick",
    )

    def after(value, *ties):
        return lax.optimization_barrier((value, *ties))[0]

    def hop(piece, *ties, last=False):
        up, down = piece
        front, back, *_ = lax.optimization_barrier((up[-1], down[-1], *ties))
        if last:
            front, back = front[: HALF // 2], back[HALF // 2 :]
        up.append(shifted(front, "z", 1))
        down.append(shifted(back, "z", -1))

    a, b = [([gated[lo : lo + HALF]], [gated[lo : lo + HALF]]) for lo in (0, HALF)]
    hop(a)
    hop(b)
    hop(a)
    far = swapped(far, 2)
    hop(b)
    near = swapped(near, 1)
    hop(a, far)
    next_far = shifted(far, "core", 1)
    hop(b, near)
    next_near = shifted(near, "core", 1)
    hop(a, next_far, last=True)
    weight = call(
        weight_kernel,
        shape((z_size * chans, y_size * chans), bf16),
        [],
        out_weight.size,
        (by_owner, near, next_near, far, next_far),
        "weights",
    )
    hop(b, weight, last=True)

    def project(piece, *ties):
        own, *sent = call(
            project_kernel,
            (shape((HALF, chans), f32),) + (shape((HALF, chans), bf16),) * 3,
            [],
            2 * HALF * z_size * y_size * chans * chans,
            (*piece[0], *piece[1][1:], lax.optimization_barrier((weight, *ties))[0]),
            "project",
        )
        return own, *[swapped(part, kind) for part, kind in zip(sent, KINDS)]

    return call(
        finish_kernel,
        shape((rows, chans), bf16),
        [],
        rows * chans,
        (*project(a, b[1][3]), *project(b)),
        "finish",
    )


def solution(mesh):
    ctx_size, tp_size = mesh.devices.shape
    fine = Mesh(mesh.devices.reshape(ctx_size // 2, 2, tp_size // 4, 4), ("x", "core", "z", "y"))
    tp = ("z", "y")
    in_specs = (
        P(CTX, None, tp),
        P(None, None, tp),
        P(None, tp),
        P(None, tp),
        P(tp),
        P(None, tp),
    )
    return jax.shard_map(shards, mesh=fine, in_specs=in_specs, out_specs=P(CTX, tp), check_vma=False)
```

```python
import functools
import math

import jax
import jax.numpy as jnp
from jax import lax
from jax.experimental import pallas as pl
from jax.experimental.pallas import tpu as pltpu
from jax.sharding import Mesh, PartitionSpec as P

CTX = ("x", "core")
SUB = 8
PAD = 8
UNROLL = 8
HALF = 1024
KINDS = (2, 1, 3)
LOADS = 4
BACK = (0, 2, 3, 1)
VMEM_LIMIT = 16 * 1024 * 1024
ROW_TILE = 256


def shifted(value, axis, steps):
    count = lax.axis_size(axis)
    return lax.ppermute(value, axis, [(at, (at + steps) % count) for at in range(count)])


def swapped(value, kind):
    count = lax.axis_size("y")
    pairs = []
    for core in range(2):
        flip = kind if kind == 2 or core == 0 else 4 - kind
        pairs += [(core * count + at, core * count + (at ^ flip)) for at in range(count)]
    return lax.ppermute(value, ("core", "y"), pairs)


def peers():
    core, here = lax.axis_index("core"), lax.axis_index("y")
    return {kind: here ^ (kind + core * (4 - 2 * kind)) for kind in (1, 2, 3)}


def from_behind(value, axis, steps):
    count = lax.axis_size(axis)
    return lax.ppermute(value, axis, [(at, at + steps) for at in range(count - steps)])


def wide(row):
    return jnp.broadcast_to(row, (SUB, row.shape[-1]))


def added(parts):
    while len(parts) > 1:
        pairs = [a + b for a, b in zip(parts[0::2], parts[1::2])]
        parts = pairs + parts[2 * len(pairs) :]
    return parts[0]


def widen(raw, padded_ref, first, last):
    blocks, steps, _ = raw.shape
    for c in range(blocks):
        at = c * (steps + PAD) + PAD
        padded_ref[at + first : at + last, :] = raw[c, first:last, :].astype(jnp.float32)


def lead_in(tails, padded_ref, steps):
    blocks, count, chans = tails.shape
    padded_ref[PAD - 2 : PAD, :] = jnp.zeros((2, chans), jnp.float32)
    for c in range(1, blocks):
        at = c * (steps + PAD) + PAD
        padded_ref[at - 2 : at, :] = tails[c - 1].astype(jnp.float32)[count - 2 : count, :]


def row_of(ref, step, steps):
    return ref[pl.ds(PAD + step, SUB, stride=steps + PAD), :]


def mode_rows(param_ref):
    order = (param_ref.shape[0] - 16) // 3
    taps = lambda j, s: param_ref[3 * j + s : 3 * j + s + 1, :]
    rate, decay, weight = [param_ref[16 + order * i : 16 + order * (i + 1), :] for i in range(3)]
    return taps, param_ref[9:10, :], rate, decay, weight


def state_kernel(stream_hbm, taps_hbm, rate_hbm, residue_hbm, skip_hbm, *rest):
    signal_ref, start_ref, packed_ref, param_ref, *scratch = rest
    raw_ref, tail_ref, edge_ref, taps_ref, rate_ref, residue_ref, skip_ref, key_ref, val_ref, sems = scratch
    _, blocks, steps, chans = stream_hbm.shape
    order = rate_ref.shape[0]
    pair = pl.ds(1, 2)
    part = steps // LOADS
    sources = [
        (stream_hbm.at[pair, :, pl.ds(steps - 16, 16)], tail_ref),
        (taps_hbm, taps_ref),
        (rate_hbm, rate_ref),
        (residue_hbm, residue_ref),
        (skip_hbm, skip_ref),
        (stream_hbm.at[0, 0, pl.ds(0, 16)], edge_ref.at[0]),
        (stream_hbm.at[0, blocks - 1, pl.ds(steps - 16, 16)], edge_ref.at[1]),
    ]
    for at in range(LOADS):
        span = pl.ds(at * part, part)
        sources.append((stream_hbm.at[pair, :, span], raw_ref.at[:, :, span]))
    copies = [pltpu.make_async_copy(*pair, sems.at[i]) for i, pair in enumerate(sources)]
    small, large = copies[:-LOADS], copies[-LOADS:]
    for copy in small[:3] + large + small[3:]:
        copy.start()
    for copy in small[:3]:
        copy.wait()

    for j in range(3):
        for s in range(3):
            param_ref[3 * j + s : 3 * j + s + 1, :] = taps_ref[j, s : s + 1, :]
    param_ref[10:16, :] = jnp.zeros((6, chans), jnp.float32)
    rates = rate_ref[...]
    param_ref[16 : 16 + order, :] = rates
    param_ref[16 + order : 16 + 2 * order, :] = jnp.exp(-rates)
    taps, _, _, fade, _ = mode_rows(param_ref)
    lead_in(tail_ref.at[0], key_ref, steps)
    lead_in(tail_ref.at[1], val_ref, steps)

    decay = [wide(fade[r : r + 1, :]) for r in range(order)]
    key_taps = [wide(taps(j, 1)) for j in range(3)]
    val_taps = [wide(taps(j, 2)) for j in range(3)]
    block = lax.broadcasted_iota(jnp.int32, (SUB, chans), 0)

    def advance(step, carried, masked):
        k2, k1, v2, v1, *states = carried
        k0 = row_of(key_ref, step, steps)
        v0 = row_of(val_ref, step, steps)
        key = key_taps[0] * k2 + key_taps[1] * k1 + key_taps[2] * k0
        val = val_taps[0] * v2 + val_taps[1] * v1 + val_taps[2] * v0
        signal = key * val
        if masked:
            signal = jnp.where(block == 0, 0.0, signal)
        signal_ref[step] = signal
        states = [a * h + signal for a, h in zip(decay, states)]
        return [k1, k0, v1, v0, *states]

    def body(at, carried):
        carried = list(carried)
        for step in range(UNROLL):
            carried = advance(at * UNROLL + step, carried, False)
        return tuple(carried)

    carried = [row_of(ref, step, steps) for ref in (key_ref, val_ref) for step in (-2, -1)]
    carried += [jnp.zeros((SUB, chans), jnp.float32)] * order
    for at in range(LOADS):
        large[at].wait()
        for which, ref in enumerate((key_ref, val_ref)):
            widen(raw_ref.at[which], ref, at * part, (at + 1) * part)
        begin = at * part // UNROLL
        if at == 0:
            for step in range(UNROLL):
                carried = advance(step, carried, step < 2)
            begin = 1
        carried = lax.fori_loop(begin, (at + 1) * part // UNROLL, body, tuple(carried))
    for copy in small[3:]:
        copy.wait()
    param_ref[9:10, :] = skip_ref[...]
    param_ref[16 + 2 * order : 16 + 3 * order, :] = residue_ref[...] * jnp.sqrt(2.0 * rates)
    states = carried[4:]
    for r in range(order):
        rate = wide(rates[r : r + 1, :])
        total = states[r]
        for back in (1, 2, 4):
            gain = jnp.where(block >= back, jnp.exp(-rate * (steps * back)), 0.0)
            total = total + gain * pltpu.roll(total, back, 0)
        packed_ref[r : r + 1, :] = total[SUB - 1 : SUB, :]
        start_ref[r] = jnp.where(block == 0, 0.0, pltpu.roll(total, 1, 0))
    end = blocks * (steps + PAD)
    heads = [edge_ref[0].astype(jnp.float32)[0:2, :], key_ref[PAD : PAD + 2, :], val_ref[PAD : PAD + 2, :]]
    tails = [
        edge_ref[1].astype(jnp.float32)[14:16, :],
        key_ref[end - 2 : end, :],
        val_ref[end - 2 : end, :],
    ]
    for s in range(3):
        packed_ref[order + 2 * s : order + 2 * s + 2, :] = heads[s]
        packed_ref[order + 6 + 2 * s : order + 8 + 2 * s, :] = tails[s]
    packed_ref[order + 12 :, :] = jnp.zeros((packed_ref.shape[0] - order - 12, chans), jnp.float32)


def local_steps(first, param_ref, signal_ref, start_ref, conv_ref):
    order = start_ref.shape[0]
    _, skip, _, decay, weight = mode_rows(param_ref)
    decay = [wide(decay[r : r + 1, :]) for r in range(order)]
    weight = [wide(weight[r : r + 1, :]) for r in range(order)]
    skip = wide(skip)

    def body(at, states):
        for inner in range(UNROLL):
            step = at * UNROLL + inner
            signal = signal_ref[first + step]
            states = [a * h + signal for a, h in zip(decay, states)]
            conv_ref[step] = added([w * h for w, h in zip(weight, states)] + [skip * signal])
        return tuple(states)

    states = tuple(start_ref[r] for r in range(order))
    return lax.fori_loop(0, conv_ref.shape[0] // UNROLL, body, states)


def local_kernel(param_ref, signal_ref, start_ref, conv_ref, next_ref):
    states = local_steps(0, param_ref, signal_ref, start_ref, conv_ref)
    for r, state in enumerate(states):
        next_ref[r] = state


def local_query_kernel(stream_hbm, param_ref, signal_ref, start_ref, conv_ref, query_ref, raw_ref, wide_ref, sem):
    copy = pltpu.make_async_copy(stream_hbm.at[0], raw_ref, sem)
    copy.start()
    blocks, steps, _ = raw_ref.shape
    local_steps(conv_ref.shape[0], param_ref, signal_ref, start_ref, conv_ref)
    copy.wait()
    widen(raw_ref, wide_ref, 0, steps)
    lead_in(raw_ref.at[:, pl.ds(steps - 16, 16)], wide_ref, steps)
    taps = [wide(mode_rows(param_ref)[0](j, 0)) for j in range(3)]

    def body(at, carried):
        q2, q1 = carried
        for inner in range(UNROLL):
            step = at * UNROLL + inner
            q0 = row_of(wide_ref, step, steps)
            query_ref[step] = taps[0] * q2 + taps[1] * q1 + taps[2] * q0
            q2, q1 = q1, q0
        return q2, q1

    lax.fori_loop(0, steps // UNROLL, body, (row_of(wide_ref, -2, steps), row_of(wide_ref, -1, steps)))


def pack_kernel(*refs):
    *parts, out_ref = refs
    at = 0
    for part in parts:
        count = 1 if len(part.shape) == 2 else part.shape[0]
        out_ref[at : at + count] = part[...].reshape(count, *out_ref.shape[1:])
        at += count


def gate_kernel(param_ref, query_ref, conv0_ref, conv1_ref, *rest):
    *own_refs, other_ref, out_ref, nat_ref, ends_ref = rest
    rows, chans = out_ref.shape
    steps = rows // SUB
    core = lax.axis_index("core")
    for at, (back, own_ref) in enumerate(zip(BACK, own_refs)):
        pair = 2 * (len(own_refs) - 1 - back)
        ends_ref[pair + core] = own_ref[...]
        ends_ref[pair + 1 - core] = other_ref[at]
    taps, skip, rate, decay, weight = mode_rows(param_ref)
    order = rate.shape[0]
    tap = [[taps(j, s) for s in range(3)] for j in range(3)]

    def head_feat(at, s):
        head, tail = order + 2 * s, order + 6 + 2 * s
        x0, x1 = ends_ref[at, head : head + 1, :], ends_ref[at, head + 1 : head + 2, :]
        if isinstance(at, int) and at == 0:
            m2 = m1 = jnp.zeros_like(x0)
        else:
            m2, m1 = ends_ref[at - 1, tail : tail + 1, :], ends_ref[at - 1, tail + 1 : tail + 2, :]
        first = tap[0][s] * m2 + tap[1][s] * m1 + tap[2][s] * x0
        second = tap[0][s] * m1 + tap[1][s] * x0 + tap[2][s] * x1
        return first, second

    whole = jnp.exp(-rate * rows)
    lead0 = jnp.exp(-rate * (rows - 1))
    lead1 = jnp.exp(-rate * (rows - 2))
    running = jnp.zeros((order, chans), jnp.float32)
    last = ends_ref.shape[0]
    for at in range(last):
        k0, k1 = head_feat(at, 1)
        v0, v1 = head_feat(at, 2)
        h0, h1 = head_feat(at, 0)
        now = (running, k0 * v0, k1 * v1, h0, h1)
        if at == last - 2:
            state, s0, s1, q0, q1 = now
        elif at == last - 1:
            state, s0, s1, q0, q1 = [
                jnp.where(core == 1, new, old) for new, old in zip(now, (state, s0, s1, q0, q1))
            ]
        running = whole * running + ends_ref[at, 0:order, :] + lead0 * now[1] + lead1 * now[2]
    at0 = decay * state + s0
    at1 = decay * at0 + s1
    conv0 = jnp.sum(weight * at0, axis=0, keepdims=True) + skip * s0
    conv1 = jnp.sum(weight * at1, axis=0, keepdims=True) + skip * s1

    block = lax.broadcasted_iota(jnp.int32, (SUB, chans), 0).astype(jnp.float32)
    begin = weight * at1
    decays = [wide(decay[r : r + 1, :]) for r in range(order)]
    terms = [
        wide(begin[r : r + 1, :]) * jnp.exp(-wide(rate[r : r + 1, :]) * (block * steps - 1.0))
        for r in range(order)
    ]

    terms = tuple(terms)
    for which, conv_ref in enumerate((conv0_ref, conv1_ref)):
        count = conv_ref.shape[0]

        def body(at, terms):
            for inner in range(UNROLL):
                local = at * UNROLL + inner
                step = which * count + local
                conv = added([conv_ref[local], *terms])
                nat_ref[pl.ds(step, SUB, stride=steps), :] = query_ref[step] * conv
                terms = [p * a for p, a in zip(terms, decays)]
            return tuple(terms)

        terms = lax.fori_loop(0, count // UNROLL, body, terms)
    nat_ref[0:1, :] = q0 * conv0
    nat_ref[1:2, :] = q1 * conv1
    tile = 128
    for at in range(0, rows, tile):
        out_ref[at : at + tile, :] = nat_ref[at : at + tile, :].astype(jnp.bfloat16)


def pick_kernel(by_owner_ref, near, far):
    peer = peers()
    count = far.shape[0]
    near[...] = by_owner_ref[:, peer[1]]
    far[...] = by_owner_ref[pl.ds(lax.axis_index("core") * count, count), peer[2]]


def weight_kernel(by_owner_ref, near, next_near, far, next_far, weight):
    count, _, depth, _ = by_owner_ref.shape
    half = far.shape[0]
    here, core = lax.axis_index("y"), lax.axis_index("core")
    for j in range(count):
        source = lax.rem(lax.axis_index("z") - j + count, count)
        within = lax.rem(source, half)
        mine = core * half <= source
        mine = mine & (source < core * half + half)
        far_block = jnp.where(mine, far[within], next_far[within])
        rows = slice(j * depth, (j + 1) * depth)
        for s, block in enumerate((by_owner_ref[source, here], far_block, near[source], next_near[source])):
            weight[rows, s * depth : (s + 1) * depth] = block


def project_kernel(here, f1, f2, f3, f4, b1, b2, b3, b4, weight, own, *sent):
    rows, depth = here.shape
    for start in range(0, rows, ROW_TILE):
        span = slice(start, start + ROW_TILE)
        near = [piece[span, :] for piece in (here, f1, f2, f3, b3, b2, b1)]
        half = rows // 2
        far = f4[span, :] if start < half else b4[start - half : start - half + ROW_TILE, :]
        left = jnp.concatenate([*near[:4], far, *near[4:]], axis=1)
        total = jnp.dot(left, weight[...], preferred_element_type=jnp.float32)
        own[span, :] = total[:, 0:depth]
        for s, part in enumerate(sent):
            part[span, :] = total[:, (s + 1) * depth : (s + 2) * depth].astype(jnp.bfloat16)


def finish_kernel(piece, own, one, two, three, *rest):
    *_, out_hbm, half_ref, sem = rest
    rows = own.shape[0]
    tile = 128
    for at in range(0, rows, tile):
        total = own[at : at + tile, :]
        for part in (one, two, three):
            total = total + part[at : at + tile, :].astype(jnp.float32)
        half_ref[at : at + tile, :] = total.astype(jnp.bfloat16)
    copy = pltpu.make_async_copy(half_ref, out_hbm.at[pl.ds(piece * rows, rows)], sem)
    copy.start()
    copy.wait()


def call(kernel, shapes, scratch, flops, args, name, limit=VMEM_LIMIT, **more):
    arrays = [*args, *jax.tree.leaves(shapes, is_leaf=lambda s: hasattr(s, "dtype"))]
    size = sum(math.prod(a.shape) * jnp.dtype(a.dtype).itemsize for a in arrays)
    return pl.pallas_call(
        kernel,
        out_shape=shapes,
        scratch_shapes=scratch,
        compiler_params=pltpu.CompilerParams(vmem_limit_bytes=limit),
        cost_estimate=pl.CostEstimate(flops=flops, bytes_accessed=size, transcendentals=0),
        name=name,
        **more,
    )(*args)


def shards(streams, short_filter, residue, decay_rate, skip_gain, out_weight):
    f32, bf16 = jnp.float32, jnp.bfloat16
    rows, _, chans = streams.shape
    order = residue.shape[0]
    steps = rows // SUB
    z_size, y_size = lax.axis_size("z"), lax.axis_size("y")
    shape = jax.ShapeDtypeStruct

    vmem = pl.BlockSpec(memory_space=pltpu.VMEM)
    def in_hbm(value):
        return pltpu.with_memory_space_constraint(value, pltpu.HBM)

    hbm = pl.BlockSpec(memory_space=pltpu.HBM)
    planes = in_hbm(jnp.transpose(streams, (1, 0, 2)).reshape(3, SUB, steps, chans))
    padded = pltpu.VMEM((SUB * (steps + PAD), chans), f32)
    modes = [in_hbm(m) for m in (short_filter, decay_rate, residue, skip_gain[None, :])]
    signal, start, packed, params = call(
        state_kernel,
        (
            pltpu.VMEM((steps, SUB, chans), f32),
            pltpu.VMEM((order, SUB, chans), f32),
            pltpu.VMEM((order + 16, chans), f32),
            pltpu.VMEM((16 + 3 * order, chans), f32),
        ),
        [
            pltpu.VMEM((2, SUB, steps, chans), bf16),
            pltpu.VMEM((2, SUB, 16, chans), bf16),
            pltpu.VMEM((2, 16, chans), bf16),
            *[pltpu.VMEM(m.shape, f32) for m in modes],
            padded,
            padded,
            pltpu.SemaphoreType.DMA((7 + LOADS,)),
        ],
        rows * chans * 44,
        (planes, *modes),
        "states",
        in_specs=[hbm] * 5,
        out_specs=(vmem,) * 4,
    )
    half_steps = pltpu.VMEM((steps // 2, SUB, chans), f32)
    past = {back: from_behind(packed, "x", back) for back in BACK[1:]}
    conv0, middle = call(
        local_kernel,
        (half_steps, pltpu.VMEM((order, SUB, chans), f32)),
        [],
        rows * chans * 33,
        (params, signal, start),
        "local_conv",
        in_specs=[vmem] * 3,
        out_specs=(vmem,) * 2,
    )
    conv1, query = call(
        local_query_kernel,
        (half_steps, pltpu.VMEM((steps, SUB, chans), f32)),
        [pltpu.VMEM((SUB, steps, chans), bf16), padded, pltpu.SemaphoreType.DMA],
        rows * chans * 40,
        (planes, params, signal, middle),
        "local_conv_query",
        in_specs=[hbm] + [vmem] * 3,
        out_specs=(vmem,) * 2,
    )
    own_ends, _ = lax.optimization_barrier(((packed, *[past[back] for back in BACK[1:]]), conv1))
    ends = call(
        pack_kernel, shape((len(own_ends), *packed.shape), f32), [], 4 * packed.size, own_ends, "pack"
    )
    other_ends = shifted(ends, "core", 1)
    gated = call(
        gate_kernel,
        shape((rows, chans), bf16),
        [pltpu.VMEM((rows, chans), f32), pltpu.VMEM((8, *packed.shape), f32)],
        rows * chans * 34,
        (params, query, conv0, conv1, *own_ends, other_ends),
        "gate",
        in_specs=[vmem] * 9,
        out_specs=vmem,
    )

    by_owner = out_weight.reshape(z_size, y_size, chans, chans)
    near, far = call(
        pick_kernel,
        (shape((z_size, chans, chans), bf16), shape((z_size // 2, chans, chans), bf16)),
        [],
        out_weight.size,
        (lax.optimization_barrier((by_owner, gated))[0],),
        "pick",
    )

    def after(value, *ties):
        return lax.optimization_barrier((value, *ties))[0]

    def hop(piece, *ties, last=False):
        up, down = piece
        front, back, *_ = lax.optimization_barrier((up[-1], down[-1], *ties))
        if last:
            front, back = front[: HALF // 2], back[HALF // 2 :]
        up.append(shifted(front, "z", 1))
        down.append(shifted(back, "z", -1))

    a, b = [([gated[lo : lo + HALF]], [gated[lo : lo + HALF]]) for lo in (0, HALF)]
    hop(a)
    hop(b)
    hop(a)
    far = swapped(far, 2)
    hop(b)
    near = swapped(near, 1)
    hop(a, far)
    next_far = shifted(far, "core", 1)
    hop(b, near)
    next_near = shifted(near, "core", 1)
    hop(a, next_far, last=True)
    weight = call(
        weight_kernel,
        shape((z_size * chans, y_size * chans), bf16),
        [],
        out_weight.size,
        (by_owner, near, next_near, far, next_far),
        "weights",
    )
    hop(b, weight, last=True)

    def project(piece, *ties):
        own, *sent = call(
            project_kernel,
            (shape((HALF, chans), f32),) + (shape((HALF, chans), bf16),) * 3,
            [],
            2 * HALF * z_size * y_size * chans * chans,
            (*piece[0], *piece[1][1:], lax.optimization_barrier((weight, *ties))[0]),
            "project",
        )
        return own, *[swapped(part, kind) for part, kind in zip(sent, KINDS)]

    def finish(piece, parts, *earlier):
        earlier = tuple(in_hbm(e) for e in earlier)
        return call(
            functools.partial(finish_kernel, piece),
            pltpu.HBM((rows, chans), bf16),
            [pltpu.VMEM((HALF, chans), bf16), pltpu.SemaphoreType.DMA],
            HALF * chans,
            (*parts, *earlier),
            "finish",
            in_specs=[vmem] * 4 + [hbm] * len(earlier),
            out_specs=hbm,
            input_output_aliases={4 + at: at for at in range(len(earlier))},
        )

    first = project(b)
    second = project(a, b[1][3])
    return finish(0, second, finish(1, first))


def solution(mesh):
    ctx_size, tp_size = mesh.devices.shape
    fine = Mesh(mesh.devices.reshape(ctx_size // 2, 2, tp_size // 4, 4), ("x", "core", "z", "y"))
    tp = ("z", "y")
    in_specs = (
        P(CTX, None, tp),
        P(None, None, tp),
        P(None, tp),
        P(None, tp),
        P(tp),
        P(None, tp),
    )
    return jax.shard_map(shards, mesh=fine, in_specs=in_specs, out_specs=P(CTX, tp), check_vma=False)
```

```python
import functools
import math

import jax
import jax.numpy as jnp
from jax import lax
from jax.experimental import pallas as pl
from jax.experimental.pallas import tpu as pltpu
from jax.sharding import Mesh, PartitionSpec as P

CTX = ("x", "core")
SUB = 8
PAD = 8
UNROLL = 16
HALF = 1024
KINDS = (2, 1, 3)
LOADS = 4
BACK = (0, 2, 3, 1)
VMEM_LIMIT = 16 * 1024 * 1024
ROW_TILE = 256


def shifted(value, axis, steps):
    count = lax.axis_size(axis)
    return lax.ppermute(value, axis, [(at, (at + steps) % count) for at in range(count)])


def swapped(value, kind):
    count = lax.axis_size("y")
    pairs = []
    for core in range(2):
        flip = kind if kind == 2 or core == 0 else 4 - kind
        pairs += [(core * count + at, core * count + (at ^ flip)) for at in range(count)]
    return lax.ppermute(value, ("core", "y"), pairs)


def peers():
    core, here = lax.axis_index("core"), lax.axis_index("y")
    return {kind: here ^ (kind + core * (4 - 2 * kind)) for kind in (1, 2, 3)}


def from_behind(value, axis, steps):
    count = lax.axis_size(axis)
    return lax.ppermute(value, axis, [(at, at + steps) for at in range(count - steps)])


def wide(row):
    return jnp.broadcast_to(row, (SUB, row.shape[-1]))


def added(parts):
    while len(parts) > 1:
        pairs = [a + b for a, b in zip(parts[0::2], parts[1::2])]
        parts = pairs + parts[2 * len(pairs) :]
    return parts[0]


def widen(raw, padded_ref, first, last):
    blocks, steps, _ = raw.shape
    for c in range(blocks):
        at = c * (steps + PAD) + PAD
        padded_ref[at + first : at + last, :] = raw[c, first:last, :].astype(jnp.float32)


def lead_in(tails, padded_ref, steps):
    blocks, count, chans = tails.shape
    padded_ref[PAD - 2 : PAD, :] = jnp.zeros((2, chans), jnp.float32)
    for c in range(1, blocks):
        at = c * (steps + PAD) + PAD
        padded_ref[at - 2 : at, :] = tails[c - 1].astype(jnp.float32)[count - 2 : count, :]


def row_of(ref, step, steps):
    return ref[pl.ds(PAD + step, SUB, stride=steps + PAD), :]


def mode_rows(param_ref):
    order = (param_ref.shape[0] - 16) // 3
    taps = lambda j, s: param_ref[3 * j + s : 3 * j + s + 1, :]
    rate, decay, weight = [param_ref[16 + order * i : 16 + order * (i + 1), :] for i in range(3)]
    return taps, param_ref[9:10, :], rate, decay, weight


def state_kernel(stream_hbm, taps_hbm, rate_hbm, residue_hbm, skip_hbm, *rest):
    signal_ref, start_ref, packed_ref, param_ref, *scratch = rest
    raw_ref, tail_ref, edge_ref, taps_ref, rate_ref, residue_ref, skip_ref, key_ref, val_ref, sems = scratch
    _, blocks, steps, chans = stream_hbm.shape
    order = rate_ref.shape[0]
    pair = pl.ds(1, 2)
    part = steps // LOADS
    sources = [
        (stream_hbm.at[pair, :, pl.ds(steps - 16, 16)], tail_ref),
        (taps_hbm, taps_ref),
        (rate_hbm, rate_ref),
        (residue_hbm, residue_ref),
        (skip_hbm, skip_ref),
        (stream_hbm.at[0, 0, pl.ds(0, 16)], edge_ref.at[0]),
        (stream_hbm.at[0, blocks - 1, pl.ds(steps - 16, 16)], edge_ref.at[1]),
    ]
    for at in range(LOADS):
        span = pl.ds(at * part, part)
        sources.append((stream_hbm.at[pair, :, span], raw_ref.at[:, :, span]))
    copies = [pltpu.make_async_copy(*pair, sems.at[i]) for i, pair in enumerate(sources)]
    small, large = copies[:-LOADS], copies[-LOADS:]
    for copy in small[:3] + large + small[3:]:
        copy.start()
    for copy in small[:3]:
        copy.wait()

    for j in range(3):
        for s in range(3):
            param_ref[3 * j + s : 3 * j + s + 1, :] = taps_ref[j, s : s + 1, :]
    param_ref[10:16, :] = jnp.zeros((6, chans), jnp.float32)
    rates = rate_ref[...]
    param_ref[16 : 16 + order, :] = rates
    param_ref[16 + order : 16 + 2 * order, :] = jnp.exp(-rates)
    taps, _, _, fade, _ = mode_rows(param_ref)
    lead_in(tail_ref.at[0], key_ref, steps)
    lead_in(tail_ref.at[1], val_ref, steps)

    decay = [wide(fade[r : r + 1, :]) for r in range(order)]
    key_taps = [wide(taps(j, 1)) for j in range(3)]
    val_taps = [wide(taps(j, 2)) for j in range(3)]
    block = lax.broadcasted_iota(jnp.int32, (SUB, chans), 0)

    def advance(step, carried, masked):
        k2, k1, v2, v1, *states = carried
        k0 = row_of(key_ref, step, steps)
        v0 = row_of(val_ref, step, steps)
        key = key_taps[0] * k2 + key_taps[1] * k1 + key_taps[2] * k0
        val = val_taps[0] * v2 + val_taps[1] * v1 + val_taps[2] * v0
        signal = key * val
        if masked:
            signal = jnp.where(block == 0, 0.0, signal)
        signal_ref[step] = signal
        states = [a * h + signal for a, h in zip(decay, states)]
        return [k1, k0, v1, v0, *states]

    def body(at, carried):
        carried = list(carried)
        for step in range(UNROLL):
            carried = advance(at * UNROLL + step, carried, False)
        return tuple(carried)

    carried = [row_of(ref, step, steps) for ref in (key_ref, val_ref) for step in (-2, -1)]
    carried += [jnp.zeros((SUB, chans), jnp.float32)] * order
    for at in range(LOADS):
        large[at].wait()
        for which, ref in enumerate((key_ref, val_ref)):
            widen(raw_ref.at[which], ref, at * part, (at + 1) * part)
        begin = at * part // UNROLL
        if at == 0:
            for step in range(UNROLL):
                carried = advance(step, carried, step < 2)
            begin = 1
        carried = lax.fori_loop(begin, (at + 1) * part // UNROLL, body, tuple(carried))
    for copy in small[3:]:
        copy.wait()
    param_ref[9:10, :] = skip_ref[...]
    param_ref[16 + 2 * order : 16 + 3 * order, :] = residue_ref[...] * jnp.sqrt(2.0 * rates)
    states = carried[4:]
    for r in range(order):
        rate = wide(rates[r : r + 1, :])
        total = states[r]
        for back in (1, 2, 4):
            gain = jnp.where(block >= back, jnp.exp(-rate * (steps * back)), 0.0)
            total = total + gain * pltpu.roll(total, back, 0)
        packed_ref[r : r + 1, :] = total[SUB - 1 : SUB, :]
        start_ref[r] = jnp.where(block == 0, 0.0, pltpu.roll(total, 1, 0))
    end = blocks * (steps + PAD)
    heads = [edge_ref[0].astype(jnp.float32)[0:2, :], key_ref[PAD : PAD + 2, :], val_ref[PAD : PAD + 2, :]]
    tails = [
        edge_ref[1].astype(jnp.float32)[14:16, :],
        key_ref[end - 2 : end, :],
        val_ref[end - 2 : end, :],
    ]
    for s in range(3):
        packed_ref[order + 2 * s : order + 2 * s + 2, :] = heads[s]
        packed_ref[order + 6 + 2 * s : order + 8 + 2 * s, :] = tails[s]
    packed_ref[order + 12 :, :] = jnp.zeros((packed_ref.shape[0] - order - 12, chans), jnp.float32)


def local_steps(first, param_ref, signal_ref, start_ref, conv_ref):
    order = start_ref.shape[0]
    _, skip, _, decay, weight = mode_rows(param_ref)
    decay = [wide(decay[r : r + 1, :]) for r in range(order)]
    weight = [wide(weight[r : r + 1, :]) for r in range(order)]
    skip = wide(skip)

    def body(at, states):
        for inner in range(UNROLL):
            step = at * UNROLL + inner
            signal = signal_ref[first + step]
            states = [a * h + signal for a, h in zip(decay, states)]
            conv_ref[step] = added([w * h for w, h in zip(weight, states)] + [skip * signal])
        return tuple(states)

    states = tuple(start_ref[r] for r in range(order))
    return lax.fori_loop(0, conv_ref.shape[0] // UNROLL, body, states)


def local_kernel(param_ref, signal_ref, start_ref, conv_ref, next_ref):
    states = local_steps(0, param_ref, signal_ref, start_ref, conv_ref)
    for r, state in enumerate(states):
        next_ref[r] = state


def local_query_kernel(stream_hbm, param_ref, signal_ref, start_ref, conv_ref, query_ref, raw_ref, wide_ref, sem):
    copy = pltpu.make_async_copy(stream_hbm.at[0], raw_ref, sem)
    copy.start()
    blocks, steps, _ = raw_ref.shape
    local_steps(conv_ref.shape[0], param_ref, signal_ref, start_ref, conv_ref)
    copy.wait()
    widen(raw_ref, wide_ref, 0, steps)
    lead_in(raw_ref.at[:, pl.ds(steps - 16, 16)], wide_ref, steps)
    taps = [wide(mode_rows(param_ref)[0](j, 0)) for j in range(3)]

    def body(at, carried):
        q2, q1 = carried
        for inner in range(UNROLL):
            step = at * UNROLL + inner
            q0 = row_of(wide_ref, step, steps)
            query_ref[step] = taps[0] * q2 + taps[1] * q1 + taps[2] * q0
            q2, q1 = q1, q0
        return q2, q1

    lax.fori_loop(0, steps // UNROLL, body, (row_of(wide_ref, -2, steps), row_of(wide_ref, -1, steps)))


def pack_kernel(*refs):
    *parts, out_ref = refs
    at = 0
    for part in parts:
        count = 1 if len(part.shape) == 2 else part.shape[0]
        out_ref[at : at + count] = part[...].reshape(count, *out_ref.shape[1:])
        at += count


def gate_kernel(param_ref, query_ref, conv0_ref, conv1_ref, *rest):
    *own_refs, other_ref, out_ref, nat_ref, ends_ref = rest
    rows, chans = out_ref.shape
    steps = rows // SUB
    core = lax.axis_index("core")
    for at, (back, own_ref) in enumerate(zip(BACK, own_refs)):
        pair = 2 * (len(own_refs) - 1 - back)
        ends_ref[pair + core] = own_ref[...]
        ends_ref[pair + 1 - core] = other_ref[at]
    taps, skip, rate, decay, weight = mode_rows(param_ref)
    order = rate.shape[0]
    tap = [[taps(j, s) for s in range(3)] for j in range(3)]

    def head_feat(at, s):
        head, tail = order + 2 * s, order + 6 + 2 * s
        x0, x1 = ends_ref[at, head : head + 1, :], ends_ref[at, head + 1 : head + 2, :]
        if isinstance(at, int) and at == 0:
            m2 = m1 = jnp.zeros_like(x0)
        else:
            m2, m1 = ends_ref[at - 1, tail : tail + 1, :], ends_ref[at - 1, tail + 1 : tail + 2, :]
        first = tap[0][s] * m2 + tap[1][s] * m1 + tap[2][s] * x0
        second = tap[0][s] * m1 + tap[1][s] * x0 + tap[2][s] * x1
        return first, second

    whole = jnp.exp(-rate * rows)
    lead0 = jnp.exp(-rate * (rows - 1))
    lead1 = jnp.exp(-rate * (rows - 2))
    running = jnp.zeros((order, chans), jnp.float32)
    last = ends_ref.shape[0]
    for at in range(last):
        k0, k1 = head_feat(at, 1)
        v0, v1 = head_feat(at, 2)
        h0, h1 = head_feat(at, 0)
        now = (running, k0 * v0, k1 * v1, h0, h1)
        if at == last - 2:
            state, s0, s1, q0, q1 = now
        elif at == last - 1:
            state, s0, s1, q0, q1 = [
                jnp.where(core == 1, new, old) for new, old in zip(now, (state, s0, s1, q0, q1))
            ]
        running = whole * running + ends_ref[at, 0:order, :] + lead0 * now[1] + lead1 * now[2]
    at0 = decay * state + s0
    at1 = decay * at0 + s1
    conv0 = jnp.sum(weight * at0, axis=0, keepdims=True) + skip * s0
    conv1 = jnp.sum(weight * at1, axis=0, keepdims=True) + skip * s1

    block = lax.broadcasted_iota(jnp.int32, (SUB, chans), 0).astype(jnp.float32)
    begin = weight * at1
    decays = [wide(decay[r : r + 1, :]) for r in range(order)]
    terms = [
        wide(begin[r : r + 1, :]) * jnp.exp(-wide(rate[r : r + 1, :]) * (block * steps - 1.0))
        for r in range(order)
    ]

    terms = tuple(terms)
    for which, conv_ref in enumerate((conv0_ref, conv1_ref)):
        count = conv_ref.shape[0]

        def body(at, terms):
            for inner in range(UNROLL):
                local = at * UNROLL + inner
                step = which * count + local
                conv = added([conv_ref[local], *terms])
                nat_ref[pl.ds(step, SUB, stride=steps), :] = query_ref[step] * conv
                terms = [p * a for p, a in zip(terms, decays)]
            return tuple(terms)

        terms = lax.fori_loop(0, count // UNROLL, body, terms)
    nat_ref[0:1, :] = q0 * conv0
    nat_ref[1:2, :] = q1 * conv1
    tile = 128
    for at in range(0, rows, tile):
        out_ref[at : at + tile, :] = nat_ref[at : at + tile, :].astype(jnp.bfloat16)


def pick_kernel(by_owner_ref, near, far):
    peer = peers()
    count = far.shape[0]
    near[...] = by_owner_ref[:, peer[1]]
    far[...] = by_owner_ref[pl.ds(lax.axis_index("core") * count, count), peer[2]]


def weight_kernel(by_owner_ref, near, next_near, far, next_far, weight):
    count, _, depth, _ = by_owner_ref.shape
    half = far.shape[0]
    here, core = lax.axis_index("y"), lax.axis_index("core")
    for j in range(count):
        source = lax.rem(lax.axis_index("z") - j + count, count)
        within = lax.rem(source, half)
        mine = core * half <= source
        mine = mine & (source < core * half + half)
        far_block = jnp.where(mine, far[within], next_far[within])
        rows = slice(j * depth, (j + 1) * depth)
        for s, block in enumerate((by_owner_ref[source, here], far_block, near[source], next_near[source])):
            weight[rows, s * depth : (s + 1) * depth] = block


def project_kernel(here, f1, f2, f3, f4, b1, b2, b3, b4, weight, own, *sent):
    rows, depth = here.shape
    for start in range(0, rows, ROW_TILE):
        span = slice(start, start + ROW_TILE)
        near = [piece[span, :] for piece in (here, f1, f2, f3, b3, b2, b1)]
        half = rows // 2
        far = f4[span, :] if start < half else b4[start - half : start - half + ROW_TILE, :]
        left = jnp.concatenate([*near[:4], far, *near[4:]], axis=1)
        total = jnp.dot(left, weight[...], preferred_element_type=jnp.float32)
        own[span, :] = total[:, 0:depth]
        for s, part in enumerate(sent):
            part[span, :] = total[:, (s + 1) * depth : (s + 2) * depth].astype(jnp.bfloat16)


def finish_kernel(piece, own, one, two, three, *rest):
    *_, out_hbm, half_ref, sem = rest
    rows = own.shape[0]
    tile = 128
    for at in range(0, rows, tile):
        total = own[at : at + tile, :]
        for part in (one, two, three):
            total = total + part[at : at + tile, :].astype(jnp.float32)
        half_ref[at : at + tile, :] = total.astype(jnp.bfloat16)
    copy = pltpu.make_async_copy(half_ref, out_hbm.at[pl.ds(piece * rows, rows)], sem)
    copy.start()
    copy.wait()


def call(kernel, shapes, scratch, flops, args, name, limit=VMEM_LIMIT, **more):
    arrays = [*args, *jax.tree.leaves(shapes, is_leaf=lambda s: hasattr(s, "dtype"))]
    size = sum(math.prod(a.shape) * jnp.dtype(a.dtype).itemsize for a in arrays)
    return pl.pallas_call(
        kernel,
        out_shape=shapes,
        scratch_shapes=scratch,
        compiler_params=pltpu.CompilerParams(vmem_limit_bytes=limit),
        cost_estimate=pl.CostEstimate(flops=flops, bytes_accessed=size, transcendentals=0),
        name=name,
        **more,
    )(*args)


def shards(streams, short_filter, residue, decay_rate, skip_gain, out_weight):
    f32, bf16 = jnp.float32, jnp.bfloat16
    rows, _, chans = streams.shape
    order = residue.shape[0]
    steps = rows // SUB
    z_size, y_size = lax.axis_size("z"), lax.axis_size("y")
    shape = jax.ShapeDtypeStruct

    vmem = pl.BlockSpec(memory_space=pltpu.VMEM)
    def in_hbm(value):
        return pltpu.with_memory_space_constraint(value, pltpu.HBM)

    hbm = pl.BlockSpec(memory_space=pltpu.HBM)
    planes = in_hbm(jnp.transpose(streams, (1, 0, 2)).reshape(3, SUB, steps, chans))
    padded = pltpu.VMEM(((SUB + 1) * (steps + PAD), chans), f32)
    modes = [in_hbm(m) for m in (short_filter, decay_rate, residue, skip_gain[None, :])]
    signal, start, packed, params = call(
        state_kernel,
        (
            pltpu.VMEM((steps, SUB, chans), f32),
            pltpu.VMEM((order, SUB, chans), f32),
            pltpu.VMEM((order + 16, chans), f32),
            pltpu.VMEM((16 + 3 * order, chans), f32),
        ),
        [
            pltpu.VMEM((2, SUB, steps, chans), bf16),
            pltpu.VMEM((2, SUB, 16, chans), bf16),
            pltpu.VMEM((2, 16, chans), bf16),
            *[pltpu.VMEM(m.shape, f32) for m in modes],
            padded,
            padded,
            pltpu.SemaphoreType.DMA((7 + LOADS,)),
        ],
        rows * chans * 44,
        (planes, *modes),
        "states",
        in_specs=[hbm] * 5,
        out_specs=(vmem,) * 4,
    )
    half_steps = pltpu.VMEM((steps // 2, SUB, chans), f32)
    past = {back: from_behind(packed, "x", back) for back in BACK[1:]}
    conv0, middle = call(
        local_kernel,
        (half_steps, pltpu.VMEM((order, SUB, chans), f32)),
        [],
        rows * chans * 33,
        (params, signal, start),
        "local_conv",
        in_specs=[vmem] * 3,
        out_specs=(vmem,) * 2,
    )
    conv1, query = call(
        local_query_kernel,
        (half_steps, pltpu.VMEM((steps, SUB, chans), f32)),
        [pltpu.VMEM((SUB, steps, chans), bf16), padded, pltpu.SemaphoreType.DMA],
        rows * chans * 40,
        (planes, params, signal, middle),
        "local_conv_query",
        in_specs=[hbm] + [vmem] * 3,
        out_specs=(vmem,) * 2,
    )
    own_ends, _ = lax.optimization_barrier(((packed, *[past[back] for back in BACK[1:]]), conv1))
    ends = call(
        pack_kernel, shape((len(own_ends), *packed.shape), f32), [], 4 * packed.size, own_ends, "pack"
    )
    other_ends = shifted(ends, "core", 1)
    gated = call(
        gate_kernel,
        shape((rows, chans), bf16),
        [pltpu.VMEM((rows + steps, chans), f32), pltpu.VMEM((8, *packed.shape), f32)],
        rows * chans * 34,
        (params, query, conv0, conv1, *own_ends, other_ends),
        "gate",
        in_specs=[vmem] * 9,
        out_specs=vmem,
    )

    by_owner = out_weight.reshape(z_size, y_size, chans, chans)
    near, far = call(
        pick_kernel,
        (shape((z_size, chans, chans), bf16), shape((z_size // 2, chans, chans), bf16)),
        [],
        out_weight.size,
        (lax.optimization_barrier((by_owner, gated))[0],),
        "pick",
    )

    def after(value, *ties):
        return lax.optimization_barrier((value, *ties))[0]

    def hop(piece, *ties, last=False):
        up, down = piece
        front, back, *_ = lax.optimization_barrier((up[-1], down[-1], *ties))
        if last:
            front, back = front[: HALF // 2], back[HALF // 2 :]
        up.append(shifted(front, "z", 1))
        down.append(shifted(back, "z", -1))

    a, b = [([gated[lo : lo + HALF]], [gated[lo : lo + HALF]]) for lo in (0, HALF)]
    hop(a)
    hop(b)
    hop(a)
    far = swapped(far, 2)
    hop(b)
    near = swapped(near, 1)
    hop(a, far)
    next_far = shifted(far, "core", 1)
    hop(b, near)
    next_near = shifted(near, "core", 1)
    hop(a, next_far, last=True)
    weight = call(
        weight_kernel,
        shape((z_size * chans, y_size * chans), bf16),
        [],
        out_weight.size,
        (by_owner, near, next_near, far, next_far),
        "weights",
    )
    hop(b, weight, last=True)

    def project(piece, *ties):
        own, *sent = call(
            project_kernel,
            (shape((HALF, chans), f32),) + (shape((HALF, chans), bf16),) * 3,
            [],
            2 * HALF * z_size * y_size * chans * chans,
            (*piece[0], *piece[1][1:], lax.optimization_barrier((weight, *ties))[0]),
            "project",
        )
        return own, *[swapped(part, kind) for part, kind in zip(sent, KINDS)]

    def finish(piece, parts, *earlier):
        earlier = tuple(in_hbm(e) for e in earlier)
        return call(
            functools.partial(finish_kernel, piece),
            pltpu.HBM((rows, chans), bf16),
            [pltpu.VMEM((HALF, chans), bf16), pltpu.SemaphoreType.DMA],
            HALF * chans,
            (*parts, *earlier),
            "finish",
            in_specs=[vmem] * 4 + [hbm] * len(earlier),
            out_specs=hbm,
            input_output_aliases={4 + at: at for at in range(len(earlier))},
        )

    first = project(b)
    second = project(a, b[1][3])
    return finish(0, second, finish(1, first))


def solution(mesh):
    ctx_size, tp_size = mesh.devices.shape
    fine = Mesh(mesh.devices.reshape(ctx_size // 2, 2, tp_size // 4, 4), ("x", "core", "z", "y"))
    tp = ("z", "y")
    in_specs = (
        P(CTX, None, tp),
        P(None, None, tp),
        P(None, tp),
        P(None, tp),
        P(tp),
        P(None, tp),
    )
    return jax.shard_map(shards, mesh=fine, in_specs=in_specs, out_specs=P(CTX, tp), check_vma=False)
```

```python
import functools
import math

import jax
import jax.numpy as jnp
from jax import lax
from jax.experimental import pallas as pl
from jax.experimental.pallas import tpu as pltpu
from jax.sharding import Mesh, PartitionSpec as P

CTX = ("x", "core")
SUB = 8
PAD = 8
UNROLL = 16
HALF = 1024
KINDS = (2, 1, 3)
LOADS = 4
BACK = (0, 2, 3, 1)
VMEM_LIMIT = 16 * 1024 * 1024
ROW_TILE = 512


def shifted(value, axis, steps):
    count = lax.axis_size(axis)
    return lax.ppermute(value, axis, [(at, (at + steps) % count) for at in range(count)])


def swapped(value, kind):
    count = lax.axis_size("y")
    pairs = []
    for core in range(2):
        flip = kind if kind == 2 or core == 0 else 4 - kind
        pairs += [(core * count + at, core * count + (at ^ flip)) for at in range(count)]
    return lax.ppermute(value, ("core", "y"), pairs)


def peers():
    core, here = lax.axis_index("core"), lax.axis_index("y")
    return {kind: here ^ (kind + core * (4 - 2 * kind)) for kind in (1, 2, 3)}


def from_behind(value, axis, steps):
    count = lax.axis_size(axis)
    return lax.ppermute(value, axis, [(at, at + steps) for at in range(count - steps)])


def wide(row):
    return jnp.broadcast_to(row, (SUB, row.shape[-1]))


def added(parts):
    while len(parts) > 1:
        pairs = [a + b for a, b in zip(parts[0::2], parts[1::2])]
        parts = pairs + parts[2 * len(pairs) :]
    return parts[0]


def widen(raw, padded_ref, first, last):
    blocks, steps, _ = raw.shape
    for c in range(blocks):
        at = c * (steps + PAD) + PAD
        padded_ref[at + first : at + last, :] = raw[c, first:last, :].astype(jnp.float32)


def lead_in(tails, padded_ref, steps):
    blocks, count, chans = tails.shape
    padded_ref[PAD - 2 : PAD, :] = jnp.zeros((2, chans), jnp.float32)
    for c in range(1, blocks):
        at = c * (steps + PAD) + PAD
        padded_ref[at - 2 : at, :] = tails[c - 1].astype(jnp.float32)[count - 2 : count, :]


def row_of(ref, step, steps):
    return ref[pl.ds(PAD + step, SUB, stride=steps + PAD), :]


def mode_rows(param_ref):
    order = (param_ref.shape[0] - 16) // 3
    taps = lambda j, s: param_ref[3 * j + s : 3 * j + s + 1, :]
    rate, decay, weight = [param_ref[16 + order * i : 16 + order * (i + 1), :] for i in range(3)]
    return taps, param_ref[9:10, :], rate, decay, weight


def state_kernel(stream_hbm, taps_hbm, rate_hbm, residue_hbm, skip_hbm, *rest):
    signal_ref, start_ref, packed_ref, param_ref, *scratch = rest
    raw_ref, tail_ref, edge_ref, taps_ref, rate_ref, residue_ref, skip_ref, key_ref, val_ref, sems = scratch
    _, blocks, steps, chans = stream_hbm.shape
    order = rate_ref.shape[0]
    pair = pl.ds(1, 2)
    part = steps // LOADS
    sources = [
        (stream_hbm.at[pair, :, pl.ds(steps - 16, 16)], tail_ref),
        (taps_hbm, taps_ref),
        (rate_hbm, rate_ref),
        (residue_hbm, residue_ref),
        (skip_hbm, skip_ref),
        (stream_hbm.at[0, 0, pl.ds(0, 16)], edge_ref.at[0]),
        (stream_hbm.at[0, blocks - 1, pl.ds(steps - 16, 16)], edge_ref.at[1]),
    ]
    for at in range(LOADS):
        span = pl.ds(at * part, part)
        sources.append((stream_hbm.at[pair, :, span], raw_ref.at[:, :, span]))
    copies = [pltpu.make_async_copy(*pair, sems.at[i]) for i, pair in enumerate(sources)]
    small, large = copies[:-LOADS], copies[-LOADS:]
    for copy in small[:3] + large + small[3:]:
        copy.start()
    for copy in small[:3]:
        copy.wait()

    for j in range(3):
        for s in range(3):
            param_ref[3 * j + s : 3 * j + s + 1, :] = taps_ref[j, s : s + 1, :]
    param_ref[10:16, :] = jnp.zeros((6, chans), jnp.float32)
    rates = rate_ref[...]
    param_ref[16 : 16 + order, :] = rates
    param_ref[16 + order : 16 + 2 * order, :] = jnp.exp(-rates)
    taps, _, _, fade, _ = mode_rows(param_ref)
    lead_in(tail_ref.at[0], key_ref, steps)
    lead_in(tail_ref.at[1], val_ref, steps)

    decay = [wide(fade[r : r + 1, :]) for r in range(order)]
    key_taps = [wide(taps(j, 1)) for j in range(3)]
    val_taps = [wide(taps(j, 2)) for j in range(3)]
    block = lax.broadcasted_iota(jnp.int32, (SUB, chans), 0)

    def advance(step, carried, masked):
        k2, k1, v2, v1, *states = carried
        k0 = row_of(key_ref, step, steps)
        v0 = row_of(val_ref, step, steps)
        key = key_taps[0] * k2 + key_taps[1] * k1 + key_taps[2] * k0
        val = val_taps[0] * v2 + val_taps[1] * v1 + val_taps[2] * v0
        signal = key * val
        if masked:
            signal = jnp.where(block == 0, 0.0, signal)
        signal_ref[step] = signal
        states = [a * h + signal for a, h in zip(decay, states)]
        return [k1, k0, v1, v0, *states]

    def body(at, carried):
        carried = list(carried)
        for step in range(UNROLL):
            carried = advance(at * UNROLL + step, carried, False)
        return tuple(carried)

    carried = [row_of(ref, step, steps) for ref in (key_ref, val_ref) for step in (-2, -1)]
    carried += [jnp.zeros((SUB, chans), jnp.float32)] * order
    for at in range(LOADS):
        large[at].wait()
        for which, ref in enumerate((key_ref, val_ref)):
            widen(raw_ref.at[which], ref, at * part, (at + 1) * part)
        begin = at * part // UNROLL
        if at == 0:
            for step in range(UNROLL):
                carried = advance(step, carried, step < 2)
            begin = 1
        carried = lax.fori_loop(begin, (at + 1) * part // UNROLL, body, tuple(carried))
    for copy in small[3:]:
        copy.wait()
    param_ref[9:10, :] = skip_ref[...]
    param_ref[16 + 2 * order : 16 + 3 * order, :] = residue_ref[...] * jnp.sqrt(2.0 * rates)
    states = carried[4:]
    for r in range(order):
        rate = wide(rates[r : r + 1, :])
        total = states[r]
        for back in (1, 2, 4):
            gain = jnp.where(block >= back, jnp.exp(-rate * (steps * back)), 0.0)
            total = total + gain * pltpu.roll(total, back, 0)
        packed_ref[r : r + 1, :] = total[SUB - 1 : SUB, :]
        start_ref[r] = jnp.where(block == 0, 0.0, pltpu.roll(total, 1, 0))
    end = blocks * (steps + PAD)
    heads = [edge_ref[0].astype(jnp.float32)[0:2, :], key_ref[PAD : PAD + 2, :], val_ref[PAD : PAD + 2, :]]
    tails = [
        edge_ref[1].astype(jnp.float32)[14:16, :],
        key_ref[end - 2 : end, :],
        val_ref[end - 2 : end, :],
    ]
    for s in range(3):
        packed_ref[order + 2 * s : order + 2 * s + 2, :] = heads[s]
        packed_ref[order + 6 + 2 * s : order + 8 + 2 * s, :] = tails[s]
    packed_ref[order + 12 :, :] = jnp.zeros((packed_ref.shape[0] - order - 12, chans), jnp.float32)


def local_steps(first, param_ref, signal_ref, start_ref, conv_ref):
    order = start_ref.shape[0]
    _, skip, _, decay, weight = mode_rows(param_ref)
    decay = [wide(decay[r : r + 1, :]) for r in range(order)]
    weight = [wide(weight[r : r + 1, :]) for r in range(order)]
    skip = wide(skip)

    def body(at, states):
        for inner in range(UNROLL):
            step = at * UNROLL + inner
            signal = signal_ref[first + step]
            states = [a * h + signal for a, h in zip(decay, states)]
            conv_ref[step] = added([w * h for w, h in zip(weight, states)] + [skip * signal])
        return tuple(states)

    states = tuple(start_ref[r] for r in range(order))
    return lax.fori_loop(0, conv_ref.shape[0] // UNROLL, body, states)


def local_kernel(param_ref, signal_ref, start_ref, conv_ref, next_ref):
    states = local_steps(0, param_ref, signal_ref, start_ref, conv_ref)
    for r, state in enumerate(states):
        next_ref[r] = state


def local_query_kernel(stream_hbm, param_ref, signal_ref, start_ref, conv_ref, query_ref, raw_ref, wide_ref, sem):
    copy = pltpu.make_async_copy(stream_hbm.at[0], raw_ref, sem)
    copy.start()
    blocks, steps, _ = raw_ref.shape
    local_steps(conv_ref.shape[0], param_ref, signal_ref, start_ref, conv_ref)
    copy.wait()
    widen(raw_ref, wide_ref, 0, steps)
    lead_in(raw_ref.at[:, pl.ds(steps - 16, 16)], wide_ref, steps)
    taps = [wide(mode_rows(param_ref)[0](j, 0)) for j in range(3)]

    def body(at, carried):
        q2, q1 = carried
        for inner in range(UNROLL):
            step = at * UNROLL + inner
            q0 = row_of(wide_ref, step, steps)
            query_ref[step] = taps[0] * q2 + taps[1] * q1 + taps[2] * q0
            q2, q1 = q1, q0
        return q2, q1

    lax.fori_loop(0, steps // UNROLL, body, (row_of(wide_ref, -2, steps), row_of(wide_ref, -1, steps)))


def pack_kernel(*refs):
    *parts, out_ref = refs
    at = 0
    for part in parts:
        count = 1 if len(part.shape) == 2 else part.shape[0]
        out_ref[at : at + count] = part[...].reshape(count, *out_ref.shape[1:])
        at += count


def gate_kernel(param_ref, query_ref, conv0_ref, conv1_ref, *rest):
    *own_refs, other_ref, out_ref, nat_ref, ends_ref = rest
    rows, chans = out_ref.shape
    steps = rows // SUB
    core = lax.axis_index("core")
    for at, (back, own_ref) in enumerate(zip(BACK, own_refs)):
        pair = 2 * (len(own_refs) - 1 - back)
        ends_ref[pair + core] = own_ref[...]
        ends_ref[pair + 1 - core] = other_ref[at]
    taps, skip, rate, decay, weight = mode_rows(param_ref)
    order = rate.shape[0]
    tap = [[taps(j, s) for s in range(3)] for j in range(3)]

    def head_feat(at, s):
        head, tail = order + 2 * s, order + 6 + 2 * s
        x0, x1 = ends_ref[at, head : head + 1, :], ends_ref[at, head + 1 : head + 2, :]
        if isinstance(at, int) and at == 0:
            m2 = m1 = jnp.zeros_like(x0)
        else:
            m2, m1 = ends_ref[at - 1, tail : tail + 1, :], ends_ref[at - 1, tail + 1 : tail + 2, :]
        first = tap[0][s] * m2 + tap[1][s] * m1 + tap[2][s] * x0
        second = tap[0][s] * m1 + tap[1][s] * x0 + tap[2][s] * x1
        return first, second

    whole = jnp.exp(-rate * rows)
    lead0 = jnp.exp(-rate * (rows - 1))
    lead1 = jnp.exp(-rate * (rows - 2))
    running = jnp.zeros((order, chans), jnp.float32)
    last = ends_ref.shape[0]
    for at in range(last):
        k0, k1 = head_feat(at, 1)
        v0, v1 = head_feat(at, 2)
        h0, h1 = head_feat(at, 0)
        now = (running, k0 * v0, k1 * v1, h0, h1)
        if at == last - 2:
            state, s0, s1, q0, q1 = now
        elif at == last - 1:
            state, s0, s1, q0, q1 = [
                jnp.where(core == 1, new, old) for new, old in zip(now, (state, s0, s1, q0, q1))
            ]
        running = whole * running + ends_ref[at, 0:order, :] + lead0 * now[1] + lead1 * now[2]
    at0 = decay * state + s0
    at1 = decay * at0 + s1
    conv0 = jnp.sum(weight * at0, axis=0, keepdims=True) + skip * s0
    conv1 = jnp.sum(weight * at1, axis=0, keepdims=True) + skip * s1

    block = lax.broadcasted_iota(jnp.int32, (SUB, chans), 0).astype(jnp.float32)
    begin = weight * at1
    decays = [wide(decay[r : r + 1, :]) for r in range(order)]
    terms = [
        wide(begin[r : r + 1, :]) * jnp.exp(-wide(rate[r : r + 1, :]) * (block * steps - 1.0))
        for r in range(order)
    ]

    terms = tuple(terms)
    for which, conv_ref in enumerate((conv0_ref, conv1_ref)):
        count = conv_ref.shape[0]

        def body(at, terms):
            for inner in range(UNROLL):
                local = at * UNROLL + inner
                step = which * count + local
                conv = added([conv_ref[local], *terms])
                nat_ref[pl.ds(step, SUB, stride=steps), :] = query_ref[step] * conv
                terms = [p * a for p, a in zip(terms, decays)]
            return tuple(terms)

        terms = lax.fori_loop(0, count // UNROLL, body, terms)
    nat_ref[0:1, :] = q0 * conv0
    nat_ref[1:2, :] = q1 * conv1
    tile = 128
    for at in range(0, rows, tile):
        out_ref[at : at + tile, :] = nat_ref[at : at + tile, :].astype(jnp.bfloat16)


def pick_kernel(by_owner_ref, near, far):
    peer = peers()
    count = far.shape[0]
    near[...] = by_owner_ref[:, peer[1]]
    far[...] = by_owner_ref[pl.ds(lax.axis_index("core") * count, count), peer[2]]


def weight_kernel(by_owner_ref, near, next_near, far, next_far, weight):
    count, _, depth, _ = by_owner_ref.shape
    half = far.shape[0]
    here, core = lax.axis_index("y"), lax.axis_index("core")
    for j in range(count):
        source = lax.rem(lax.axis_index("z") - j + count, count)
        within = lax.rem(source, half)
        mine = core * half <= source
        mine = mine & (source < core * half + half)
        far_block = jnp.where(mine, far[within], next_far[within])
        rows = slice(j * depth, (j + 1) * depth)
        for s, block in enumerate((by_owner_ref[source, here], far_block, near[source], next_near[source])):
            weight[rows, s * depth : (s + 1) * depth] = block


def project_kernel(here, f1, f2, f3, f4, b1, b2, b3, b4, weight, own, *sent):
    rows, depth = here.shape
    for start in range(0, rows, ROW_TILE):
        span = slice(start, start + ROW_TILE)
        near = [piece[span, :] for piece in (here, f1, f2, f3, b3, b2, b1)]
        half = rows // 2
        far = f4[span, :] if start < half else b4[start - half : start - half + ROW_TILE, :]
        left = jnp.concatenate([*near[:4], far, *near[4:]], axis=1)
        total = jnp.dot(left, weight[...], preferred_element_type=jnp.float32)
        own[span, :] = total[:, 0:depth]
        for s, part in enumerate(sent):
            part[span, :] = total[:, (s + 1) * depth : (s + 2) * depth].astype(jnp.bfloat16)


def finish_kernel(piece, own, one, two, three, *rest):
    *_, out_hbm, half_ref, sem = rest
    rows = own.shape[0]
    tile = 128
    for at in range(0, rows, tile):
        total = own[at : at + tile, :]
        for part in (one, two, three):
            total = total + part[at : at + tile, :].astype(jnp.float32)
        half_ref[at : at + tile, :] = total.astype(jnp.bfloat16)
    copy = pltpu.make_async_copy(half_ref, out_hbm.at[pl.ds(piece * rows, rows)], sem)
    copy.start()
    copy.wait()


def call(kernel, shapes, scratch, flops, args, name, limit=VMEM_LIMIT, **more):
    arrays = [*args, *jax.tree.leaves(shapes, is_leaf=lambda s: hasattr(s, "dtype"))]
    size = sum(math.prod(a.shape) * jnp.dtype(a.dtype).itemsize for a in arrays)
    return pl.pallas_call(
        kernel,
        out_shape=shapes,
        scratch_shapes=scratch,
        compiler_params=pltpu.CompilerParams(vmem_limit_bytes=limit),
        cost_estimate=pl.CostEstimate(flops=flops, bytes_accessed=size, transcendentals=0),
        name=name,
        **more,
    )(*args)


def shards(streams, short_filter, residue, decay_rate, skip_gain, out_weight):
    f32, bf16 = jnp.float32, jnp.bfloat16
    rows, _, chans = streams.shape
    order = residue.shape[0]
    steps = rows // SUB
    z_size, y_size = lax.axis_size("z"), lax.axis_size("y")
    shape = jax.ShapeDtypeStruct

    vmem = pl.BlockSpec(memory_space=pltpu.VMEM)
    def in_hbm(value):
        return pltpu.with_memory_space_constraint(value, pltpu.HBM)

    hbm = pl.BlockSpec(memory_space=pltpu.HBM)
    planes = in_hbm(jnp.transpose(streams, (1, 0, 2)).reshape(3, SUB, steps, chans))
    padded = pltpu.VMEM(((SUB + 1) * (steps + PAD), chans), f32)
    modes = [in_hbm(m) for m in (short_filter, decay_rate, residue, skip_gain[None, :])]
    signal, start, packed, params = call(
        state_kernel,
        (
            pltpu.VMEM((steps, SUB, chans), f32),
            pltpu.VMEM((order, SUB, chans), f32),
            pltpu.VMEM((order + 16, chans), f32),
            pltpu.VMEM((16 + 3 * order, chans), f32),
        ),
        [
            pltpu.VMEM((2, SUB, steps, chans), bf16),
            pltpu.VMEM((2, SUB, 16, chans), bf16),
            pltpu.VMEM((2, 16, chans), bf16),
            *[pltpu.VMEM(m.shape, f32) for m in modes],
            padded,
            padded,
            pltpu.SemaphoreType.DMA((7 + LOADS,)),
        ],
        rows * chans * 44,
        (planes, *modes),
        "states",
        in_specs=[hbm] * 5,
        out_specs=(vmem,) * 4,
    )
    half_steps = pltpu.VMEM((steps // 2, SUB, chans), f32)
    past = {back: from_behind(packed, "x", back) for back in BACK[1:]}
    conv0, middle = call(
        local_kernel,
        (half_steps, pltpu.VMEM((order, SUB, chans), f32)),
        [],
        rows * chans * 33,
        (params, signal, start),
        "local_conv",
        in_specs=[vmem] * 3,
        out_specs=(vmem,) * 2,
    )
    conv1, query = call(
        local_query_kernel,
        (half_steps, pltpu.VMEM((steps, SUB, chans), f32)),
        [pltpu.VMEM((SUB, steps, chans), bf16), padded, pltpu.SemaphoreType.DMA],
        rows * chans * 40,
        (planes, params, signal, middle),
        "local_conv_query",
        in_specs=[hbm] + [vmem] * 3,
        out_specs=(vmem,) * 2,
    )
    own_ends, _ = lax.optimization_barrier(((packed, *[past[back] for back in BACK[1:]]), conv1))
    ends = call(
        pack_kernel, shape((len(own_ends), *packed.shape), f32), [], 4 * packed.size, own_ends, "pack"
    )
    other_ends = shifted(ends, "core", 1)
    gated = call(
        gate_kernel,
        shape((rows, chans), bf16),
        [pltpu.VMEM((rows + steps, chans), f32), pltpu.VMEM((8, *packed.shape), f32)],
        rows * chans * 34,
        (params, query, conv0, conv1, *own_ends, other_ends),
        "gate",
        in_specs=[vmem] * 9,
        out_specs=vmem,
    )

    by_owner = out_weight.reshape(z_size, y_size, chans, chans)
    near, far = call(
        pick_kernel,
        (shape((z_size, chans, chans), bf16), shape((z_size // 2, chans, chans), bf16)),
        [],
        out_weight.size,
        (lax.optimization_barrier((by_owner, gated))[0],),
        "pick",
    )

    def after(value, *ties):
        return lax.optimization_barrier((value, *ties))[0]

    def hop(piece, *ties, last=False):
        up, down = piece
        front, back, *_ = lax.optimization_barrier((up[-1], down[-1], *ties))
        if last:
            front, back = front[: HALF // 2], back[HALF // 2 :]
        up.append(shifted(front, "z", 1))
        down.append(shifted(back, "z", -1))

    a, b = [([gated[lo : lo + HALF]], [gated[lo : lo + HALF]]) for lo in (0, HALF)]
    hop(a)
    hop(b)
    hop(a)
    far = swapped(far, 2)
    hop(b)
    near = swapped(near, 1)
    hop(a, far)
    next_far = shifted(far, "core", 1)
    hop(b, near)
    next_near = shifted(near, "core", 1)
    hop(a, next_far, last=True)
    weight = call(
        weight_kernel,
        shape((z_size * chans, y_size * chans), bf16),
        [],
        out_weight.size,
        (by_owner, near, next_near, far, next_far),
        "weights",
    )
    hop(b, weight, last=True)

    def project(piece, *ties):
        own, *sent = call(
            project_kernel,
            (shape((HALF, chans), f32),) + (shape((HALF, chans), bf16),) * 3,
            [],
            2 * HALF * z_size * y_size * chans * chans,
            (*piece[0], *piece[1][1:], lax.optimization_barrier((weight, *ties))[0]),
            "project",
        )
        return own, *[swapped(part, kind) for part, kind in zip(sent, KINDS)]

    def finish(piece, parts, *earlier):
        earlier = tuple(in_hbm(e) for e in earlier)
        return call(
            functools.partial(finish_kernel, piece),
            pltpu.HBM((rows, chans), bf16),
            [pltpu.VMEM((HALF, chans), bf16), pltpu.SemaphoreType.DMA],
            HALF * chans,
            (*parts, *earlier),
            "finish",
            in_specs=[vmem] * 4 + [hbm] * len(earlier),
            out_specs=hbm,
            input_output_aliases={4 + at: at for at in range(len(earlier))},
        )

    first = project(b)
    second = project(a, b[1][3])
    return finish(0, second, finish(1, first))


def solution(mesh):
    ctx_size, tp_size = mesh.devices.shape
    fine = Mesh(mesh.devices.reshape(ctx_size // 2, 2, tp_size // 4, 4), ("x", "core", "z", "y"))
    tp = ("z", "y")
    in_specs = (
        P(CTX, None, tp),
        P(None, None, tp),
        P(None, tp),
        P(None, tp),
        P(tp),
        P(None, tp),
    )
    return jax.shard_map(shards, mesh=fine, in_specs=in_specs, out_specs=P(CTX, tp), check_vma=False)
```
